32 devices in a mesh: parts: 2 (over y), fsdp: 4 (over z), member: 2 (over x), dp: 2 (over core).
Axes of the slice: x: 2, y: 2, z: 4, core: 2. Of those that a mesh axis runs over, the one named last changes fastest.
Arguments:
- skip_stream: bfloat16 [40, 512, 5120], P(('parts', 'member'), ('fsdp', 'dp')), parts along dimension 0
- projected_output_adjoint: bfloat16 [40, 512, 1024], P(('parts', 'member'), ('fsdp', 'dp')), parts along dimension 0, may hold values from -12 to 12
- frozen_projection_kernel: bfloat16 [5120, 1024], P('fsdp'), may hold values from -0.078125 to 0.078125
- lowering_projections: bfloat16 [5120, 512], P('fsdp', ('parts', 'member')), parts along dimension 1, may hold values from -0.078125 to 0.078125
- lifting_projections: bfloat16 [512, 1024], P(('parts', 'member')), parts along dimension 0, may hold values from -0.75 to 0.75
- normalizer_scales: float32 [5120], replicated, may hold values from 0.1 to 1.9
- tile_assignee: int32 [40], P(('parts', 'member')), parts along dimension 0, may hold values from 0 to 4, as said below
Outputs:
- residual_grad: bfloat16 [40, 512, 5120], P(('parts', 'member'), ('fsdp', 'dp')), parts along dimension 0
- grad_down: float32 [5120, 512], P(('fsdp', 'dp'), ('parts', 'member')), parts along dimension 1
- raising_factor_sensitivity: float32 [512, 1024], P(('parts', 'member'), ('fsdp', 'dp')), parts along dimension 0
The draws below stay inside these ranges and needn't reach their ends.
There are 2 independent parts, one for each index of `parts`. The reference program is written for one: setup_inputs(seed, part) draws one part's arguments, and reference() takes and returns one part's arrays. A program takes and returns all parts, laid end to end along the dimension named above; an argument that names none is the same for every part. Nothing has to cross between parts.
Inputs may be any that keep to these rules, and one draw needn't show every extreme that they name: `tile_assignee`: slots m*10 to (m+1)*10 - 1 hold members m*2 to (m+1)*2 - 1 or padding (4); in each such group the live slots come first, in runs of increasing member, and every member has at least one slot.
All inputs are finite; a program needn't handle non-finite values.
Results may differ from the reference program's by a relative error of at most 0.0051.
Values may be sent and summed in bfloat16 or wider, within the bound.
No kernel may reach another device: no remote copies, remote signals or barrier semaphores. Data moves between devices by JAX's collectives and lax.ppermute only.
A program may use at most 128 MiB of HBM per device.

```python
import math
import jax
import jax.numpy as jnp
from jax import lax

MODEL_WIDTH = 5120
PROJ_OUT_DIM = 1024
LOW_DIM = 64
BLOCK = 512
MEM_DEV = 2
SLOT_DEV = 10
ENSEMBLE_SIZE = 4
SLOTS = 20


def draw_skip_stream(key, part):
    key = jax.random.fold_in(key, 5)
    key_noise, key_rows, key_cols = jax.random.split(key, 3)
    tensor_dimensions = (SLOTS, BLOCK, MODEL_WIDTH)
    noise_field = jax.random.normal(key_noise, tensor_dimensions, jnp.float32)
    row_scale = jnp.exp(jax.random.uniform(key_rows, (SLOTS, BLOCK, 1), jnp.float32, math.log(0.3), math.log(3.0)))
    col_scale = jnp.exp(jax.random.uniform(key_cols, (1, 1, MODEL_WIDTH), jnp.float32, math.log(0.3), math.log(3.0)))
    return (noise_field * row_scale * col_scale).astype(jnp.bfloat16)


def draw_tile_assignee(key, part):
    key = jax.random.fold_in(key, 17)
    key_live, key_full, key_sparse, key_cuts = jax.random.split(key, 4)
    groups = SLOTS // SLOT_DEV
    group_ids = jnp.arange(groups, dtype=jnp.int32)
    live_total = jax.random.randint(key_live, (groups,), MEM_DEV, SLOT_DEV + 1)
    full_group = (2 * jax.random.randint(key_full, (), 0, groups) + jnp.asarray(part, jnp.int32)) % groups
    sparse_group = (full_group + 1 + jax.random.randint(key_sparse, (), 0, groups - 1)) % groups
    live_total = jnp.where(group_ids == full_group, SLOT_DEV, live_total)
    live_total = jnp.where(group_ids == sparse_group, MEM_DEV, live_total)
    cut_draws = jax.random.randint(key_cuts, (groups, MEM_DEV - 1), 0, (live_total - MEM_DEV + 1)[:, None])
    starts = jnp.sort(cut_draws, axis=1) + jnp.arange(1, MEM_DEV, dtype=jnp.int32)[None, :]
    positions = jnp.arange(SLOT_DEV, dtype=jnp.int32)
    local_member = jnp.sum((positions[None, :, None] >= starts[:, None, :]).astype(jnp.int32), axis=2)
    member = group_ids[:, None] * MEM_DEV + local_member
    chosen = jnp.where(positions[None, :] < live_total[:, None], member, ENSEMBLE_SIZE)
    return chosen.reshape(SLOTS).astype(jnp.int32)


def shard_levels(key, dims, shards, low, top_value):
    level, own = 1.0, jax.random.fold_in(key, 6)
    for axis_at, parts in shards:
        draws = jnp.exp(jax.random.uniform(jax.random.fold_in(own, axis_at), (parts,), jnp.float32, low / len(shards), top_value / len(shards)))
        level = level * jnp.repeat(draws, dims[axis_at] // parts).reshape([-1 if axis == axis_at else 1 for axis in range(len(dims))])
    return level


def scatter_about(own_key, shape, deviation, most, cuts=(), kind=jnp.bfloat16):
    loudness = shard_levels(own_key, shape, cuts, -0.22, 0.18) if cuts else 1.0
    result = jax.random.normal(own_key, shape, jnp.float32) * deviation * loudness
    return jnp.minimum(jnp.maximum(result, -most), most).astype(kind)


def setup_inputs(seed: int = 0, part: int = 0) -> dict:
    streams_of = jax.random.split(jax.random.key(seed), 8)
    part_splits = jax.random.split(jax.random.fold_in(streams_of[7], part), 8)
    return {
        "skip_stream": draw_skip_stream(jax.random.fold_in(jax.random.fold_in(streams_of[7], part), 71), part),
        "projected_output_adjoint": scatter_about(part_splits[1], (SLOTS, BLOCK, PROJ_OUT_DIM), 2.0, 12.0, ((0, 2), (1, 8))),
        "frozen_projection_kernel": scatter_about(streams_of[2], (MODEL_WIDTH, PROJ_OUT_DIM), MODEL_WIDTH ** -0.5, 0.078125, ((0, 4),)),
        "lowering_projections": scatter_about(part_splits[3], (MODEL_WIDTH, ENSEMBLE_SIZE * LOW_DIM), MODEL_WIDTH ** -0.5, 0.078125, ((0, 4), (1, 2))),
        "lifting_projections": scatter_about(part_splits[4], (ENSEMBLE_SIZE * LOW_DIM, PROJ_OUT_DIM), LOW_DIM ** -0.5, 0.75, ((0, 2),)),
        "normalizer_scales": jnp.clip(1.0 + 0.18 * jax.random.normal(streams_of[5], (MODEL_WIDTH,), jnp.float32), 0.1, 1.9),
        "tile_assignee": draw_tile_assignee(jax.random.fold_in(jax.random.fold_in(streams_of[7], part), 71), part),
    }


epsilon = 1e-06

def reference(skip_stream, projected_output_adjoint, frozen_projection_kernel, lowering_projections, lifting_projections, normalizer_scales, tile_assignee):
    member_ids = jnp.arange(ENSEMBLE_SIZE, dtype=jnp.int32)
    block_count = lax.optimization_barrier(jnp.sum((tile_assignee[:, None] == member_ids[None, :]).astype(jnp.float32), axis=0))

    def one_block(totals, incoming_activations):
        sum_down, sum_up = totals
        resid_block, grad_block, member = incoming_activations
        block_live = member < ENSEMBLE_SIZE
        leading_lane_start = (jnp.minimum(member, ENSEMBLE_SIZE - 1) * LOW_DIM).astype(jnp.int32)
        filtered_sensitivity_lines = jnp.where(block_live, grad_block, jnp.zeros_like(grad_block))
        widened = resid_block.astype(jnp.float32)
        root_mean = jnp.sqrt(lax.optimization_barrier(jnp.mean(widened * widened, axis=-1, keepdims=True)) + epsilon)
        normed = widened / root_mean
        hidden = (normed * normalizer_scales).astype(jnp.bfloat16)
        base_part = jnp.dot(filtered_sensitivity_lines, frozen_projection_kernel.T, preferred_element_type=jnp.float32).astype(jnp.bfloat16)
        down_member_slice = lax.dynamic_slice_in_dim(lowering_projections, leading_lane_start, LOW_DIM, 1)
        lifting_portion = lax.dynamic_slice_in_dim(lifting_projections, leading_lane_start, LOW_DIM, 0)
        middle_product = jnp.dot(filtered_sensitivity_lines, lifting_portion.T, preferred_element_type=jnp.float32).astype(jnp.bfloat16)
        projected = jnp.dot(hidden, down_member_slice, preferred_element_type=jnp.float32).astype(jnp.bfloat16)
        hidden_grad = base_part.astype(jnp.float32) + jnp.dot(middle_product, down_member_slice.T, preferred_element_type=jnp.float32)
        scaled = hidden_grad * normalizer_scales
        residual_grad = ((scaled - normed * lax.optimization_barrier(jnp.mean(scaled * normed, axis=-1, keepdims=True))) / root_mean).astype(jnp.bfloat16)
        term_down = jnp.dot(hidden.T, middle_product, preferred_element_type=jnp.float32)
        term_up = jnp.dot(projected.T, filtered_sensitivity_lines, preferred_element_type=jnp.float32)
        sum_down = lax.dynamic_update_slice_in_dim(sum_down, lax.dynamic_slice_in_dim(sum_down, leading_lane_start, LOW_DIM, 1) + term_down, leading_lane_start, 1)
        sum_up = lax.dynamic_update_slice_in_dim(sum_up, lax.dynamic_slice_in_dim(sum_up, leading_lane_start, LOW_DIM, 0) + term_up, leading_lane_start, 0)
        return ((sum_down, sum_up), residual_grad)
    initial = (jnp.zeros((MODEL_WIDTH, ENSEMBLE_SIZE * LOW_DIM), jnp.float32), jnp.zeros((ENSEMBLE_SIZE * LOW_DIM, PROJ_OUT_DIM), jnp.float32))
    (sum_down, sum_up), residual_grad = lax.scan(one_block, initial, (skip_stream, projected_output_adjoint, tile_assignee))
    inverse = jnp.repeat(1.0 / (BLOCK * block_count), LOW_DIM)
    return (residual_grad, sum_down * inverse[None, :], sum_up * inverse[:, None])
```

```python
import functools

import jax
import jax.numpy as jnp
from jax import lax
from jax.experimental import pallas as pl
from jax.experimental.pallas import tpu as pltpu
from jax.sharding import PartitionSpec as P

LOW_DIM = 64
BLOCK = 512


epsilon = 1e-06

F32 = jnp.float32
BF16 = jnp.bfloat16
MIB = 1024 * 1024


def base_grad(grads, weight_rows):
    product = jnp.einsum("srk,nk->srn", grads, weight_rows, preferred_element_type=jnp.float32)
    return product.astype(jnp.bfloat16)


def per_device_any(
    skip_stream,
    projected_output_adjoint,
    frozen_projection_kernel,
    lowering_projections,
    lifting_projections,
    normalizer_scales,
    tile_assignee,
):
    within_group_indices = lifting_projections.shape[0] // LOW_DIM
    first_member = lax.axis_index("member") * within_group_indices
    member_ids = first_member + jnp.arange(within_group_indices, dtype=jnp.int32)
    onehot = tile_assignee[:, None] == member_ids[None, :]
    live_mask = jnp.any(onehot, axis=1)
    block_count = jnp.sum(onehot.astype(jnp.float32), axis=0)
    filtered_sensitivity_lines = jnp.where(
        live_mask[:, None, None], projected_output_adjoint, jnp.zeros_like(projected_output_adjoint)
    )
    column_mask = jnp.repeat(onehot, LOW_DIM, axis=1)[:, None, :]
    widened = skip_stream.astype(jnp.float32)
    root_mean = jnp.sqrt(jnp.mean(widened * widened, axis=-1, keepdims=True) + epsilon)
    normed = widened / root_mean
    hidden = (normed * normalizer_scales).astype(jnp.bfloat16)
    middle_product = jnp.einsum(
        "qgr,vr->qgv",
        filtered_sensitivity_lines,
        lifting_projections,
        preferred_element_type=jnp.float32,
    )
    middle_product = jnp.where(column_mask, middle_product, 0.0).astype(jnp.bfloat16)
    weight_full, down_full = (
        lax.all_gather(frozen_projection_kernel, "fsdp", axis=0, tiled=True),
        lax.all_gather(lowering_projections, "fsdp", axis=0, tiled=True),
    )
    base_part = base_grad(filtered_sensitivity_lines, weight_full)
    projected = jnp.einsum("srd,dm->srm", hidden, down_full, preferred_element_type=jnp.float32)
    projected = jnp.where(column_mask, projected, 0.0).astype(jnp.bfloat16)
    hidden_grad = base_part.astype(jnp.float32) + jnp.einsum(
        "srm,dm->srd", middle_product, down_full, preferred_element_type=jnp.float32
    )
    scaled = hidden_grad * normalizer_scales
    residual_grad = (
        (scaled - normed * jnp.mean(scaled * normed, axis=-1, keepdims=True)) / root_mean
    ).astype(jnp.bfloat16)
    term_down = jnp.einsum(
        "srd,srm->dm", hidden, middle_product, preferred_element_type=jnp.float32
    )
    term_up = jnp.einsum(
        "srm,srk->mk", projected, filtered_sensitivity_lines, preferred_element_type=jnp.float32
    )
    sum_down, sum_up = (
        lax.psum_scatter(term_down, ("fsdp", "dp"), scatter_dimension=0, tiled=True),
        lax.psum_scatter(term_up, ("fsdp", "dp"), scatter_dimension=1, tiled=True),
    )
    inverse = jnp.repeat(1.0 / (BLOCK * block_count), LOW_DIM)
    return (residual_grad, sum_down * inverse[None, :], sum_up * inverse[:, None])


def nt_dot(a, b):
    return lax.dot_general(a, b, (((1,), (1,)), ((), ())), preferred_element_type=F32)


def tn_dot(a, b):
    return lax.dot_general(a, b, (((0,), (0,)), ((), ())), preferred_element_type=F32)


def params(mib=48):
    return pltpu.CompilerParams(vmem_limit_bytes=mib * MIB)


def norm_kernel(slot_ref, cols_ref, skip_ref, grad_ref, up_ref, scale_ref, hidden_ref, mid_ref, live_ref, rel_ref, inv_ref):
    step = pl.program_id(0)
    slots, rows, width = skip_ref.shape
    tokens = slots * rows
    kdim = grad_ref.shape[2]
    low = up_ref.shape[0]
    wide = skip_ref[...].reshape(tokens, width).astype(F32)
    inverse = lax.rsqrt(jnp.mean(wide * wide, axis=-1, keepdims=True) + epsilon)
    inv_ref[...] = jnp.broadcast_to(inverse, inv_ref.shape)
    hidden_ref[...] = (wide * inverse * scale_ref[...]).astype(BF16)
    lane_member = lax.broadcasted_iota(jnp.int32, (rows, low), 1) // LOW_DIM
    masks = []
    for s in range(slots):
        local = slot_ref[step * slots + s]
        alive = jnp.logical_and(local >= 0, local < low // LOW_DIM)
        live_ref[s * rows : (s + 1) * rows, :] = jnp.where(alive, grad_ref[s], jnp.zeros_like(grad_ref[s]))
        masks.append(lane_member == local)
    live = live_ref[...]
    mid = nt_dot(live, up_ref[...])
    mid_ref[...] = jnp.where(jnp.concatenate(masks, axis=0), mid, 0.0).astype(BF16)
    for j in range(kdim // 128):
        at = pl.multiple_of(cols_ref[j] * 128, 128)
        rel_ref[:, j * 128 : (j + 1) * 128] = live_ref[:, pl.ds(at, 128)]


def norm_call(slots_local, cols, skip, grad, up, scales, per_step):
    count, rows, width = skip.shape
    kdim = grad.shape[2]
    low = up.shape[0]
    block = per_step * rows
    tokens = count * rows
    row_block = lambda n: pl.BlockSpec((block, n), lambda i, *_: (i, 0))
    return pl.pallas_call(
        norm_kernel,
        out_shape=(
            jax.ShapeDtypeStruct((tokens, width), BF16),
            jax.ShapeDtypeStruct((tokens, low), BF16),
            jax.ShapeDtypeStruct((tokens, kdim), BF16),
            jax.ShapeDtypeStruct((tokens, kdim), BF16),
            jax.ShapeDtypeStruct((tokens, 128), F32),
        ),
        grid_spec=pltpu.PrefetchScalarGridSpec(
            num_scalar_prefetch=2,
            grid=(count // per_step,),
            in_specs=[
                pl.BlockSpec((per_step, rows, width), lambda i, *_: (i, 0, 0)),
                pl.BlockSpec((per_step, rows, kdim), lambda i, *_: (i, 0, 0)),
                pl.BlockSpec((low, kdim), lambda i, *_: (0, 0)),
                pl.BlockSpec((1, width), lambda i, *_: (0, 0)),
            ],
            out_specs=[row_block(width), row_block(low), row_block(kdim), row_block(kdim), row_block(128)],
        ),
        compiler_params=params(),
        cost_estimate=pl.CostEstimate(flops=2 * tokens * kdim * low, bytes_accessed=2 * tokens * (2 * width + 3 * kdim), transcendentals=0),
        name="norm",
    )(slots_local, cols, skip, grad, up, scales)


def terms_kernel(slot_ref, blocks_ref, hidden_ref, mid_ref, keep_ref, other_ref, live_ref, out_ref, up_ref, proj_ref):
    k = pl.program_id(0)
    steps = pl.num_programs(0)
    half = keep_ref.shape[1]
    out_ref[0, 0] = tn_dot(mid_ref[...], hidden_ref[...])

    @pl.when(k == 0)
    def _():
        proj_ref[...] = jnp.zeros_like(proj_ref)

    down = jnp.where(k % 2 == 0, keep_ref[k // 2], other_ref[k // 2])
    proj_ref[...] += jnp.dot(hidden_ref[...], down, preferred_element_type=F32)

    @pl.when(k == steps - 1)
    def _():
        tokens, low = proj_ref.shape
        count = slot_ref.shape[0]
        rows = tokens // count
        lane_member = lax.broadcasted_iota(jnp.int32, (rows, low), 1) // LOW_DIM
        mask = jnp.concatenate([lane_member == slot_ref[s] for s in range(count)], axis=0)
        projected = jnp.where(mask, proj_ref[...], 0.0).astype(BF16)
        for j in range(steps):
            at = pl.multiple_of(blocks_ref[j] * 128, 128)
            up_ref[j % 2, j // 2] = tn_dot(projected, live_ref[:, pl.ds(at, 128)])


def terms_call(slots_local, blocks, hidden, mid, keep, other, live):
    tokens, width = hidden.shape
    low = mid.shape[1]
    fsdp, half, _ = keep.shape
    steps = 2 * fsdp
    whole = lambda a: pl.BlockSpec(a.shape, lambda k, *_: (0,) * a.ndim)
    return pl.pallas_call(
        terms_kernel,
        out_shape=(
            jax.ShapeDtypeStruct((2, fsdp, low, half), F32),
            jax.ShapeDtypeStruct((2, fsdp, low, 128), F32),
        ),
        grid_spec=pltpu.PrefetchScalarGridSpec(
            num_scalar_prefetch=2,
            grid=(steps,),
            in_specs=[
                pl.BlockSpec((tokens, half), lambda k, slot, blocks: (0, blocks[k])),
                whole(mid),
                whole(keep),
                whole(other),
                whole(live),
            ],
            out_specs=[
                pl.BlockSpec((1, 1, low, half), lambda k, *_: (k % 2, k // 2, 0, 0)),
                pl.BlockSpec((2, fsdp, low, 128), lambda k, *_: (0, 0, 0, 0)),
            ],
            scratch_shapes=[pltpu.VMEM((tokens, low), F32)],
        ),
        compiler_params=params(),
        cost_estimate=pl.CostEstimate(flops=4 * tokens * width * low, bytes_accessed=2 * tokens * width, transcendentals=0),
        name="terms",
    )(slots_local, blocks, hidden, mid, keep, other, live)


def base_own_kernel(live_ref, weight_ref, out_ref):
    out_ref[...] = nt_dot(live_ref[...], weight_ref[...]).astype(BF16)


def base_own_call(live, weight):
    tokens, kdim = live.shape
    n = weight.shape[0]
    return pl.pallas_call(
        base_own_kernel,
        out_shape=jax.ShapeDtypeStruct((tokens, n), BF16),
        grid=(n // 256,),
        in_specs=[
            pl.BlockSpec((tokens, kdim), lambda i: (0, 0)),
            pl.BlockSpec((256, kdim), lambda i: (i, 0)),
        ],
        out_specs=pl.BlockSpec((tokens, 256), lambda i: (0, i)),
        compiler_params=params(),
        cost_estimate=pl.CostEstimate(flops=2 * tokens * kdim * n, bytes_accessed=2 * (n * kdim + tokens * (n + kdim)), transcendentals=0),
        name="base_own",
    )(live, weight)


def base_kernel(rel_ref, mine_ref, theirs_ref, out_ref):
    total = None
    for part, ref in enumerate((mine_ref, theirs_ref)):
        for i in range(2):
            weight = jnp.concatenate([ref[2 * i], ref[2 * i + 1]], axis=-1)
            at = (part * 2 + i) * 256
            term = nt_dot(rel_ref[:, at : at + 256], weight)
            total = term if total is None else total + term
    out_ref[...] = total.astype(BF16)


def base_call(rel, mine, theirs):
    tokens, kdim = rel.shape
    n = mine.shape[1]
    piece = pl.BlockSpec((4, 256, 128), lambda i: (0, i, 0))
    return pl.pallas_call(
        base_kernel,
        out_shape=jax.ShapeDtypeStruct((tokens, n), BF16),
        grid=(n // 256,),
        in_specs=[pl.BlockSpec((tokens, kdim), lambda i: (0, 0)), piece, piece],
        out_specs=pl.BlockSpec((tokens, 256), lambda i: (0, i)),
        compiler_params=params(),
        cost_estimate=pl.CostEstimate(flops=2 * tokens * kdim * n, bytes_accessed=2 * (n * kdim + tokens * (n + kdim)), transcendentals=0),
        name="base",
    )(rel, mine, theirs)


def residual_kernel(blocks_ref, skip_ref, inv_ref, mid_ref, keep_ref, other_ref, scale_ref, *rest):
    *bases, out_ref, scaled_ref = rest
    slots, rows, width = skip_ref.shape
    tokens = slots * rows
    half = keep_ref.shape[1]
    inverse = inv_ref[:, :1]
    mid = mid_ref[...]
    total = jnp.zeros((tokens, 1), F32)
    for r, base_ref in enumerate(bases):
        for h in range(2):
            block = blocks_ref[2 * r + h]
            at = pl.multiple_of(block * half, 128)
            inside = pl.multiple_of((block % 2) * half, 128)
            down = (keep_ref if h == 0 else other_ref)[r]
            grad = base_ref[:, pl.ds(inside, half)].astype(F32) + nt_dot(mid, down)
            scaled = grad * scale_ref[:, pl.ds(at, half)]
            scaled_ref[:, pl.ds(at, half)] = scaled
            normed = skip_ref[:, :, pl.ds(at, half)].reshape(tokens, half).astype(F32) * inverse
            total += jnp.sum(scaled * normed, axis=-1, keepdims=True)
    mean = total * (inverse / width)
    for k in range(2 * len(bases)):
        cols = slice(k * half, (k + 1) * half)
        wide = skip_ref[:, :, cols].reshape(tokens, half).astype(F32)
        out = (scaled_ref[:, cols] - wide * mean) * inverse
        out_ref[:, :, cols] = out.astype(BF16).reshape(slots, rows, half)


def residual_call(blocks, skip, inv, mid, keep, other, scales, bases, per_step):
    count, rows, width = skip.shape
    low = mid.shape[1]
    block = per_step * rows
    n = bases[0].shape[1]
    tokens = count * rows
    row_block = lambda m: pl.BlockSpec((block, m), lambda i, *_: (i, 0))
    whole = lambda a: pl.BlockSpec(a.shape, lambda k, *_: (0,) * a.ndim)
    return pl.pallas_call(
        residual_kernel,
        out_shape=jax.ShapeDtypeStruct(skip.shape, BF16),
        grid_spec=pltpu.PrefetchScalarGridSpec(
            num_scalar_prefetch=1,
            grid=(count // per_step,),
            in_specs=[
                pl.BlockSpec((per_step, rows, width), lambda i, *_: (i, 0, 0)),
                row_block(128),
                row_block(low),
                whole(keep),
                whole(other),
                whole(scales),
            ]
            + [row_block(n)] * len(bases),
            out_specs=pl.BlockSpec((per_step, rows, width), lambda i, *_: (i, 0, 0)),
            scratch_shapes=[pltpu.VMEM((block, width), F32)],
        ),
        compiler_params=params(),
        cost_estimate=pl.CostEstimate(flops=2 * tokens * width * low, bytes_accessed=6 * tokens * width, transcendentals=0),
        name="residual",
    )(blocks, skip, inv, mid, keep, other, scales, *bases)


def finish_kernel(inv_ref, own_ref, *rest):
    *others, down_ref, up_ref = rest
    total = own_ref[0]
    for ref in others:
        total = total + ref[...].astype(F32)
    total = total * inv_ref[:, :1]
    half = down_ref.shape[0]
    down_ref[...] = total[:, :half].T
    up_ref[...] = total[:, half:]


def finish_call(inverse, own, others):
    low, both = own.shape[1:]
    half = both - 128
    return pl.pallas_call(
        finish_kernel,
        out_shape=(jax.ShapeDtypeStruct((half, low), F32), jax.ShapeDtypeStruct((low, 128), F32)),
        grid=(1,),
        in_specs=[
            pl.BlockSpec(inverse.shape, lambda i: (0, 0)),
            pl.BlockSpec((1, low, both), lambda i: (0, 0, 0)),
        ]
        + [pl.BlockSpec((low, both), lambda i: (0, 0))] * len(others),
        out_specs=[pl.BlockSpec((half, low), lambda i: (0, 0)), pl.BlockSpec((low, 128), lambda i: (0, 0))],
        compiler_params=params(),
        name="finish",
    )(inverse, own, *others)


SWAP = [(0, 1), (1, 0)]


def per_device_square(
    fsdp,
    skip,
    grad,
    weight,
    down,
    up,
    scales,
    assignee,
):
    z = lax.axis_index("fsdp")
    c = lax.axis_index("dp")
    m = lax.axis_index("member")
    piece = c * 4 + lax.axis_index("parts") * 2 + m
    half = down.shape[0] // 2
    low = up.shape[0]
    members = low // LOW_DIM

    shift = lambda v, r: lax.ppermute(v, "fsdp", [(i, (i + r) % fsdp) for i in range(fsdp)])
    over = lambda v, axis: lax.ppermute(v, axis, SWAP)

    down_half = lax.dynamic_slice_in_dim(down, c * half, half, 0)
    unit = lax.dynamic_slice_in_dim(weight, piece * 128, 128, 1)
    keep = jnp.stack([down_half] + [shift(down_half, -r) for r in range(1, fsdp)])
    other = over(keep, "dp")
    mine, theirs = [], []
    for r in range(1, fsdp):
        u = shift(unit, -r)
        ux = over(u, "member")
        uy = over(u, "parts")
        mid_row = u.shape[0] // 2
        d0 = over(ux[:mid_row], "parts")
        d1 = over(uy[mid_row:], "member")
        own = jnp.concatenate([u, ux, uy, d0, d1], axis=0).reshape(4, u.shape[0], 128)
        mine.append(own)
        theirs.append(over(own, "dp"))

    local = assignee - m * members
    cols = piece ^ jnp.arange(8, dtype=jnp.int32)
    steps = jnp.arange(2 * fsdp, dtype=jnp.int32)
    blocks = ((z + steps // 2) % fsdp) * 2 + (c ^ (steps % 2))
    scale_row = scales[None, :]

    hidden, mid, live, rel, inv = norm_call(local, cols, skip, grad, up, scale_row, 2)
    bases = [base_own_call(live, weight)]
    term_down, term_up = terms_call(local, blocks, hidden, mid, keep, other, live)
    terms = jnp.concatenate([term_down, term_up], axis=-1)
    summed = terms[0] + over(terms[1], "dp")
    sent = summed.astype(BF16)
    others = [shift(sent[r], r) for r in range(1, fsdp)]
    counts = jnp.sum((local[:, None] == jnp.arange(members)[None, :]).astype(F32), axis=0)
    inverse = jnp.repeat(1.0 / (BLOCK * counts), LOW_DIM)
    grad_down, grad_up = finish_call(jnp.broadcast_to(inverse[:, None], (low, 128)), summed, others)

    for own, far in zip(mine, theirs):
        bases.append(base_call(rel, own, far))
    residual = residual_call(blocks, skip, inv, mid, keep, other, scale_row, bases, 2)
    return residual, grad_down, grad_up


def solution(mesh):
    placed = (
        P(("parts", "member"), ("fsdp", "dp"), None),
        P(("parts", "member"), ("fsdp", "dp"), None),
        P("fsdp", None),
        P("fsdp", ("parts", "member")),
        P(("parts", "member"), None),
        P(),
        P(("parts", "member")),
    )
    sizes = dict(mesh.shape)
    square = sizes["parts"] == 2 and sizes["member"] == 2 and sizes["dp"] == 2 and sizes["fsdp"] == 4
    return jax.shard_map(
        functools.partial(per_device_square, sizes["fsdp"]) if square else per_device_any,
        mesh=mesh,
        in_specs=placed,
        out_specs=(
            P(("parts", "member"), ("fsdp", "dp"), None),
            P(("fsdp", "dp"), ("parts", "member")),
            P(("parts", "member"), ("fsdp", "dp")),
        ),
        check_vma=False,
    )
```

```python
import functools

import jax
import jax.numpy as jnp
from jax import lax
from jax.experimental import pallas as pl
from jax.experimental.pallas import tpu as pltpu
from jax.sharding import PartitionSpec as P

LOW_DIM = 64
BLOCK = 512


epsilon = 1e-06

F32 = jnp.float32
BF16 = jnp.bfloat16
MIB = 1024 * 1024


def base_grad(grads, weight_rows):
    product = jnp.einsum("srk,nk->srn", grads, weight_rows, preferred_element_type=jnp.float32)
    return product.astype(jnp.bfloat16)


def per_device_any(
    skip_stream,
    projected_output_adjoint,
    frozen_projection_kernel,
    lowering_projections,
    lifting_projections,
    normalizer_scales,
    tile_assignee,
):
    within_group_indices = lifting_projections.shape[0] // LOW_DIM
    first_member = lax.axis_index("member") * within_group_indices
    member_ids = first_member + jnp.arange(within_group_indices, dtype=jnp.int32)
    onehot = tile_assignee[:, None] == member_ids[None, :]
    live_mask = jnp.any(onehot, axis=1)
    block_count = jnp.sum(onehot.astype(jnp.float32), axis=0)
    filtered_sensitivity_lines = jnp.where(
        live_mask[:, None, None], projected_output_adjoint, jnp.zeros_like(projected_output_adjoint)
    )
    column_mask = jnp.repeat(onehot, LOW_DIM, axis=1)[:, None, :]
    widened = skip_stream.astype(jnp.float32)
    root_mean = jnp.sqrt(jnp.mean(widened * widened, axis=-1, keepdims=True) + epsilon)
    normed = widened / root_mean
    hidden = (normed * normalizer_scales).astype(jnp.bfloat16)
    middle_product = jnp.einsum(
        "qgr,vr->qgv",
        filtered_sensitivity_lines,
        lifting_projections,
        preferred_element_type=jnp.float32,
    )
    middle_product = jnp.where(column_mask, middle_product, 0.0).astype(jnp.bfloat16)
    weight_full, down_full = (
        lax.all_gather(frozen_projection_kernel, "fsdp", axis=0, tiled=True),
        lax.all_gather(lowering_projections, "fsdp", axis=0, tiled=True),
    )
    base_part = base_grad(filtered_sensitivity_lines, weight_full)
    projected = jnp.einsum("srd,dm->srm", hidden, down_full, preferred_element_type=jnp.float32)
    projected = jnp.where(column_mask, projected, 0.0).astype(jnp.bfloat16)
    hidden_grad = base_part.astype(jnp.float32) + jnp.einsum(
        "srm,dm->srd", middle_product, down_full, preferred_element_type=jnp.float32
    )
    scaled = hidden_grad * normalizer_scales
    residual_grad = (
        (scaled - normed * jnp.mean(scaled * normed, axis=-1, keepdims=True)) / root_mean
    ).astype(jnp.bfloat16)
    term_down = jnp.einsum(
        "srd,srm->dm", hidden, middle_product, preferred_element_type=jnp.float32
    )
    term_up = jnp.einsum(
        "srm,srk->mk", projected, filtered_sensitivity_lines, preferred_element_type=jnp.float32
    )
    sum_down, sum_up = (
        lax.psum_scatter(term_down, ("fsdp", "dp"), scatter_dimension=0, tiled=True),
        lax.psum_scatter(term_up, ("fsdp", "dp"), scatter_dimension=1, tiled=True),
    )
    inverse = jnp.repeat(1.0 / (BLOCK * block_count), LOW_DIM)
    return (residual_grad, sum_down * inverse[None, :], sum_up * inverse[:, None])


def nt_dot(a, b):
    return lax.dot_general(a, b, (((1,), (1,)), ((), ())), preferred_element_type=F32)


def tn_dot(a, b):
    return lax.dot_general(a, b, (((0,), (0,)), ((), ())), preferred_element_type=F32)


COST = pl.CostEstimate(flops=1000, bytes_accessed=1000, transcendentals=0)


def params(mib=20):
    return pltpu.CompilerParams(vmem_limit_bytes=mib * MIB)


def member_mask(local, rows, shape, token_axis):
    slot = lax.broadcasted_iota(jnp.int32, shape, token_axis) // rows
    column_member = lax.broadcasted_iota(jnp.int32, shape, 1 - token_axis) // LOW_DIM
    token_member = jnp.full(shape, -1, jnp.int32)
    for s, e in enumerate(local):
        token_member = jnp.where(slot == s, e, token_member)
    return token_member == column_member


HBM = pl.BlockSpec(memory_space=pltpu.HBM)
VMEM = pl.BlockSpec(memory_space=pltpu.VMEM)
SMEM = pl.BlockSpec(memory_space=pltpu.SMEM)
ROWS = 128
COLUMNS = 256


class Copies:
    def __init__(self, sems):
        self.sems = sems
        self.used = 0

    def start(self, pairs):
        group = []
        for source, target in pairs:
            copy = pltpu.make_async_copy(source, target, self.sems.at[self.used])
            self.used += 1
            copy.start()
            group.append(copy)
        return group


def wait(group):
    for copy in group:
        copy.wait()


def quarters(width):
    step = width // 4
    return [slice(q * step, (q + 1) * step) for q in range(4)]


def norm_kernel(slot_ref, skip_ref, grad_ref, up_ref, inv_ref, mid_ref, turned_ref):
    tokens, width = skip_ref.shape
    low = up_ref.shape[0]
    count = slot_ref.shape[0]
    rows = tokens // count
    for first in range(0, tokens, ROWS):
        at = slice(first, first + ROWS)
        local = [slot_ref[s] for s in range(at.start // rows, at.stop // rows)]
        across = member_mask(local, rows, (ROWS, low), 0)
        along = member_mask(local, rows, (low, ROWS), 1)
        mid_ref[at, :] = jnp.where(across, nt_dot(grad_ref[at, :], up_ref[...]), 0.0).astype(BF16)
        turned_ref[:, at] = jnp.where(along, nt_dot(up_ref[...], grad_ref[at, :]), 0.0).astype(BF16)
        totals = [jnp.zeros((ROWS, 128), F32), jnp.zeros((ROWS, 128), F32)]
        for j in range(width // 128):
            wide = skip_ref[at, j * 128 : (j + 1) * 128].astype(F32)
            totals[j % 2] += wide * wide
        mean = jnp.sum(totals[0] + totals[1], axis=-1, keepdims=True) / width
        inv_ref[at, :] = jnp.broadcast_to(lax.rsqrt(mean + epsilon), (ROWS, 128))


def norm_call(slots_local, skip, grad, up):
    tokens, width = skip.shape
    low = up.shape[0]
    return pl.pallas_call(
        norm_kernel,
        out_shape=(
            pltpu.VMEM((tokens, 128), F32),
            pltpu.VMEM((tokens, low), BF16),
            pltpu.VMEM((low, tokens), BF16),
        ),
        in_specs=[SMEM, VMEM, VMEM, VMEM],
        out_specs=[VMEM] * 3,
        compiler_params=params(),
        cost_estimate=COST,
        name="norm",
    )(slots_local, skip, grad, up)


def terms_kernel(fsdp, slot_ref, place_ref, skip_ref, grad_ref, inv_ref, scale_ref, turned_ref, own_ref, *rest):
    far_refs, rest = rest[: 2 * (fsdp - 1)], rest[2 * (fsdp - 1) :]
    keep_out, send_out, term_ref, hidden_ref, down_ref, up_ref, sems = rest
    outs = (keep_out, send_out)
    core = place_ref[0]
    tokens, width = skip_ref.shape
    n = width // fsdp
    half = n // 2
    low = turned_ref.shape[0]
    copies = Copies(sems)
    inverse = inv_ref[...]
    projected = jnp.zeros((tokens, low), F32)
    stores = []
    for r in range(fsdp):
        start = lax.rem(place_ref[1] + r, fsdp) * n
        if r == 0:
            down = own_ref[...]
        else:
            for k in range(2):
                down_ref[core ^ k] = far_refs[k * (fsdp - 1) + r - 1][...]
            down = down_ref[...].reshape(n, low)
        for j in range(n // 128):
            cols = pl.ds(pl.multiple_of(start + j * 128, 128), 128)
            hidden_ref[:, j * 128 : (j + 1) * 128] = (skip_ref[:, cols].astype(F32) * inverse * scale_ref[:, cols]).astype(BF16)
        for h in range(2):
            cols = slice(h * half, (h + 1) * half)
            term_ref[core ^ h, r, :, :half] = jnp.dot(turned_ref[...], hidden_ref[:, cols], preferred_element_type=F32)
        stores += copies.start([(term_ref.at[h, r, :, pl.ds(0, half)], outs[h].at[r, :, pl.ds(0, half)]) for h in range(2)])
        projected += jnp.dot(hidden_ref[...], down, preferred_element_type=F32)
    count = slot_ref.shape[0]
    mask = member_mask([slot_ref[s] for s in range(count)], tokens // count, (tokens, low), 0)
    projected = jnp.where(mask, projected, 0.0).astype(BF16)
    up_ref[...] = tn_dot(projected, grad_ref[...])
    for r in range(fsdp):
        shard = lax.rem(place_ref[1] + r, fsdp)
        for h in range(2):
            at = pl.multiple_of((shard * 2 + (core ^ h)) * 128, 128)
            term_ref[h, r, :, half:] = up_ref[:, pl.ds(at, 128)]
    stores += copies.start([(term_ref.at[h, :, :, pl.ds(half, 128)], outs[h].at[:, :, pl.ds(half, 128)]) for h in range(2)])
    wait(stores)


def terms_call(slots_local, place, skip, inv, scales, turned, down, keep, other, grad):
    tokens, width = skip.shape
    low = turned.shape[0]
    n = down.shape[0]
    fsdp = width // n
    both = n // 2 + 128
    out = jax.ShapeDtypeStruct((fsdp, low, both), F32)
    return pl.pallas_call(
        functools.partial(terms_kernel, fsdp),
        out_shape=(out, out),
        in_specs=[SMEM, SMEM] + [VMEM] * (6 + 2 * (fsdp - 1)),
        out_specs=[pl.BlockSpec(memory_space=pl.ANY)] * 2,
        scratch_shapes=[
            pltpu.VMEM((2, fsdp, low, both), F32),
            pltpu.VMEM((tokens, n), BF16),
            pltpu.VMEM((2, n // 2, low), BF16),
            pltpu.VMEM((low, grad.shape[1]), F32),
            pltpu.SemaphoreType.DMA((2 * fsdp + 2,)),
        ],
        compiler_params=params(),
        cost_estimate=COST,
        name="terms",
    )(slots_local, place, skip, grad, inv, scales, turned, down, *keep, *other)


def base_kernel(r, fsdp, spans, place_ref, grad_ref, mid_ref, skip_ref, scale_ref, *rest):
    *ins, out_ref, sum_ref, both_ref, weight_ref, down_ref = rest
    tokens, n = out_ref.shape
    kdim = grad_ref.shape[1]
    core = place_ref[0]
    start = lax.rem(place_ref[1] + r, fsdp) * n
    half = n // 2
    if r:
        for j in range(kdim // 128):
            at = pl.multiple_of((place_ref[2] ^ j) * 128, 128)
            both_ref[:, j * 128 : (j + 1) * 128] = grad_ref[:, pl.ds(at, 128)]
        for k in range(2):
            at = pl.multiple_of((core ^ k) * half, half)
            down_ref[pl.ds(at, half), :] = ins[len(spans) + k][...]
        for ref, (column, first, count, wide) in zip(ins, spans):
            weight_ref[first : first + count, column : column + wide] = ref[...]
    else:
        both_ref[:, :kdim] = grad_ref[...]
        down_ref[...] = ins[1][...]
    both_ref[:, kdim:] = mid_ref[...]
    total = jnp.zeros(sum_ref.shape, F32)
    for i in range(n // COLUMNS):
        rows = slice(i * COLUMNS, (i + 1) * COLUMNS)
        weight = jnp.concatenate([(weight_ref if r else ins[0])[rows, :], down_ref[rows, :]], axis=-1)
        scale = scale_ref[:, pl.ds(pl.multiple_of(start + i * COLUMNS, 128), COLUMNS)]
        scaled = nt_dot(both_ref[...], weight) * scale
        out_ref[:, rows] = scaled.astype(BF16)
        for j in range(COLUMNS // 128):
            cols = pl.ds(pl.multiple_of(start + i * COLUMNS + j * 128, 128), 128)
            total += scaled[:, j * 128 : (j + 1) * 128] * skip_ref[:, cols].astype(F32)
    sum_ref[...] = total


def base_call(r, fsdp, place, grad, mid, skip, scales, spans, ins):
    tokens, kdim = grad.shape
    low = mid.shape[1]
    n = skip.shape[1] // fsdp
    return pl.pallas_call(
        functools.partial(base_kernel, r, fsdp, spans),
        out_shape=(pltpu.VMEM((tokens, n), BF16), pltpu.VMEM((tokens, 128), F32)),
        in_specs=[SMEM] + [VMEM] * (4 + len(ins)),
        out_specs=[VMEM] * 2,
        scratch_shapes=[
            pltpu.VMEM((tokens, kdim + low), BF16),
            pltpu.VMEM((n, kdim) if r else (8, 128), BF16),
            pltpu.VMEM((n, low), BF16),
        ],
        compiler_params=params(),
        cost_estimate=COST,
        name="base",
    )(place, grad, mid, skip, scales, *ins)


def residual_kernel(fsdp, slot_ref, place_ref, skip_ref, inv_ref, *rest):
    base_refs, sum_refs, rest = rest[:fsdp], rest[fsdp : 2 * fsdp], rest[2 * fsdp :]
    out_hbm, out_ref, keep_ref, pull_ref, sems = rest
    tokens, width = skip_ref.shape
    n = width // fsdp
    rows = tokens // slot_ref.shape[0]
    copies = Copies(sems)
    inverse = inv_ref[...]
    total = sum_refs[0][...]
    for ref in sum_refs[1:]:
        total = total + ref[...]
    mean = jnp.sum(total, axis=-1, keepdims=True) * inverse / width
    pull_ref[...] = mean * inverse
    for s in range(slot_ref.shape[0]):
        local = slot_ref[s]
        alive = jnp.logical_and(local >= 0, local < place_ref[3])
        at = slice(s * rows, (s + 1) * rows)
        keep_ref[at, :] = inverse[at, :] * jnp.where(alive, 1.0, 0.0)
    stores = []
    for first in range(0, tokens, ROWS):

        def some_rows(k, carry):
            at = pl.ds(pl.multiple_of(first + k * 32, 32), 32)
            for r in range(fsdp):
                start = lax.rem(place_ref[1] + r, fsdp) * n
                for j in range(n // 128):
                    cols = pl.ds(pl.multiple_of(start + j * 128, 128), 128)
                    wide = skip_ref[at, cols].astype(F32)
                    scaled = base_refs[r][at, j * 128 : (j + 1) * 128].astype(F32)
                    out_ref[at, cols] = ((scaled - wide * pull_ref[at, :]) * keep_ref[at, :]).astype(BF16)
            return carry

        lax.fori_loop(0, ROWS // 32, some_rows, 0)
        at = pl.ds(first, ROWS)
        stores += copies.start([(out_ref.at[at, q], out_hbm.at[at, q]) for q in quarters(width)])
    wait(stores)


def residual_call(slots_local, place, skip, inv, bases, sums):
    tokens, width = skip.shape
    fsdp = len(bases)
    small = pltpu.VMEM((tokens, 128), F32)
    return pl.pallas_call(
        functools.partial(residual_kernel, fsdp),
        out_shape=jax.ShapeDtypeStruct(skip.shape, BF16),
        in_specs=[SMEM, SMEM] + [VMEM] * (2 + 2 * fsdp),
        out_specs=HBM,
        scratch_shapes=[
            pltpu.VMEM((tokens, width), BF16),
            small,
            small,
            pltpu.SemaphoreType.DMA((4 * (tokens // ROWS),)),
        ],
        compiler_params=params(),
        cost_estimate=COST,
        name="residual",
    )(slots_local, place, skip, inv, *bases, *sums)


def both_kernel(keep_ref, got_ref, own_ref, *sent_refs):
    own_ref[...] = keep_ref[0] + got_ref[0]
    for r, ref in enumerate(sent_refs, 1):
        ref[...] = (keep_ref[r] + got_ref[r]).astype(BF16)


def both_call(keep, got):
    fsdp, low, both = keep.shape
    sent = jax.ShapeDtypeStruct((low, both), BF16)
    return pl.pallas_call(
        both_kernel,
        out_shape=(jax.ShapeDtypeStruct((low, both), F32),) + (sent,) * (fsdp - 1),
        in_specs=[VMEM] * 2,
        out_specs=[VMEM] * fsdp,
        compiler_params=params(),
        cost_estimate=COST,
        name="both",
    )(keep, got)


def finish_kernel(slot_ref, own_ref, *rest):
    *others, down_ref, up_ref = rest
    total = own_ref[...]
    for ref in others:
        total = total + ref[...].astype(F32)
    low = total.shape[0]
    member = lax.broadcasted_iota(jnp.int32, (low, 128), 0) // LOW_DIM
    counts = jnp.zeros((low, 128), F32)
    for s in range(slot_ref.shape[0]):
        counts += jnp.where(member == slot_ref[s], 1.0, 0.0)
    inverse = 1.0 / (BLOCK * counts)
    half = down_ref.shape[0]
    for j in range(half // 128):
        cols = slice(j * 128, (j + 1) * 128)
        down_ref[cols, :] = (total[:, cols] * inverse).T
    up_ref[...] = total[:, half:] * inverse


def finish_call(slots_local, own, others):
    low, both = own.shape
    half = both - 128
    return pl.pallas_call(
        finish_kernel,
        out_shape=(jax.ShapeDtypeStruct((half, low), F32), jax.ShapeDtypeStruct((low, 128), F32)),
        in_specs=[SMEM] + [VMEM] * (1 + len(others)),
        out_specs=[VMEM] * 2,
        compiler_params=params(),
        cost_estimate=COST,
        name="finish",
    )(slots_local, own, *others)


SWAP = [(0, 1), (1, 0)]


def after(value, *deps):
    return lax.optimization_barrier((value, *deps))[0]


def per_device_square(
    fsdp,
    skip_stream,
    grad_stream,
    weight,
    down,
    up,
    scales,
    assignee,
):
    z = lax.axis_index("fsdp")
    c = lax.axis_index("dp")
    m = lax.axis_index("member")
    piece = c * 4 + lax.axis_index("parts") * 2 + m
    half = down.shape[0] // 2
    low = up.shape[0]
    members = low // LOW_DIM
    skip = skip_stream.reshape(-1, skip_stream.shape[2])
    grad = grad_stream.reshape(-1, grad_stream.shape[2])
    scale_row = scales[None, :]
    local = assignee - m * members
    place = jnp.stack([c, z, piece, jnp.int32(members)])

    shift = lambda v, r: lax.ppermute(v, "fsdp", [(i, (i + r) % fsdp) for i in range(fsdp)])
    over = lambda v, axis: lax.ppermute(v, axis, SWAP)
    gate = lax.optimization_barrier
    n = down.shape[0]
    kdim = grad.shape[1]
    narrow = lambda j: (j * 128, 0, n, 128)

    def base(r, g, spans, ins):
        return base_call(r, fsdp, place, g, mid, skip, scale_row, spans, ins)

    def cores(values):
        return tuple(over(v, "dp") for v in values)

    def base_far(r, g, near, far, keep, other):
        return base(r, g, tuple(narrow(j) for j in range(8)), (*near, *far, keep[r - 1], other[r - 1]))

    unit = lax.dynamic_slice_in_dim(weight, piece * 128, 128, 1)
    down_half = lax.dynamic_slice_in_dim(down, c * half, half, 0)
    u1, u3 = shift(unit, -1), shift(unit, 1)
    inv, mid, turned = norm_call(local, skip, grad, up)
    u1, u3, unit, down_half, inv, mid, turned = gate((u1, u3, unit, down_half, inv, mid, turned))

    keep = [shift(down_half, -r) for r in range(1, fsdp)]
    u2 = shift(unit, -2)
    x1, y1 = over(u1, "member"), over(u1, "parts")
    x3, y3 = over(u3, "member"), over(u3, "parts")
    base0 = base(0, grad, ((0, 0, n, kdim),), (weight, down))
    u1, u3, x1, y1, x3, y3, keep, _ = gate((u1, u3, x1, y1, x3, y3, keep, base0[1]))

    d1, d3 = over(x1, "parts"), over(y3, "member")
    other = cores(keep)
    far1, far3 = cores((u1, x1, y1)), cores((u3, x3, y3))
    terms = terms_call(local, place, skip, inv, scale_row, turned, down, keep, other, grad)
    d1, d3, far1, far3, terms, u2 = gate((d1, d3, far1, far3, terms, u2))

    own, *sent = both_call(terms[0], over(terms[1], "dp"))
    x2, y2 = over(u2, "member"), over(u2, "parts")
    far1 += cores((d1,))
    far3 += cores((d3,))
    base1 = base_far(1, grad, (u1, x1, y1, d1), far1, keep, other)
    base3 = base_far(3, grad, (u3, x3, y3, d3), far3, keep, other)
    u2, x2, y2, sent, _ = gate((u2, x2, y2, sent, base1[1] + base3[1]))

    others = [shift(v, r) for r, v in enumerate(sent, 1)]
    rows = n // 2
    d2 = (over(x2[:rows], "parts"), over(y2[rows:], "member"))
    far2 = cores((u2, x2, y2))
    d2, far2 = gate((d2, far2))

    far_d2 = cores(d2)
    spans = []
    for j in range(8):
        spans += [narrow(j)] if j % 4 < 3 else [(j * 128, at, rows, 128) for at in (0, rows)]
    base2 = base(2, grad, tuple(spans), (u2, x2, y2, *d2, *far2, *far_d2, keep[1], other[1]))
    grad_down, grad_up = finish_call(local, own, others)
    bases, sums = zip(base0, base1, base2, base3)
    residual = residual_call(local, place, skip, inv, bases, sums)
    return residual.reshape(skip_stream.shape), grad_down, grad_up


def solution(mesh):
    placed = (
        P(("parts", "member"), ("fsdp", "dp"), None),
        P(("parts", "member"), ("fsdp", "dp"), None),
        P("fsdp", None),
        P("fsdp", ("parts", "member")),
        P(("parts", "member"), None),
        P(),
        P(("parts", "member")),
    )
    sizes = dict(mesh.shape)
    square = sizes["parts"] == 2 and sizes["member"] == 2 and sizes["dp"] == 2 and sizes["fsdp"] == 4
    return jax.shard_map(
        functools.partial(per_device_square, sizes["fsdp"]) if square else per_device_any,
        mesh=mesh,
        in_specs=placed,
        out_specs=(
            P(("parts", "member"), ("fsdp", "dp"), None),
            P(("fsdp", "dp"), ("parts", "member")),
            P(("parts", "member"), ("fsdp", "dp")),
        ),
        check_vma=False,
    )
```

```python
import functools

import jax
import jax.numpy as jnp
from jax import lax
from jax.experimental import pallas as pl
from jax.experimental.pallas import tpu as pltpu
from jax.sharding import PartitionSpec as P

LOW_DIM = 64
BLOCK = 512


epsilon = 1e-06

F32 = jnp.float32
BF16 = jnp.bfloat16
MIB = 1024 * 1024


def base_grad(grads, weight_rows):
    product = jnp.einsum("srk,nk->srn", grads, weight_rows, preferred_element_type=jnp.float32)
    return product.astype(jnp.bfloat16)


def per_device_any(
    skip_stream,
    projected_output_adjoint,
    frozen_projection_kernel,
    lowering_projections,
    lifting_projections,
    normalizer_scales,
    tile_assignee,
):
    within_group_indices = lifting_projections.shape[0] // LOW_DIM
    first_member = lax.axis_index("member") * within_group_indices
    member_ids = first_member + jnp.arange(within_group_indices, dtype=jnp.int32)
    onehot = tile_assignee[:, None] == member_ids[None, :]
    live_mask = jnp.any(onehot, axis=1)
    block_count = jnp.sum(onehot.astype(jnp.float32), axis=0)
    filtered_sensitivity_lines = jnp.where(
        live_mask[:, None, None], projected_output_adjoint, jnp.zeros_like(projected_output_adjoint)
    )
    column_mask = jnp.repeat(onehot, LOW_DIM, axis=1)[:, None, :]
    widened = skip_stream.astype(jnp.float32)
    root_mean = jnp.sqrt(jnp.mean(widened * widened, axis=-1, keepdims=True) + epsilon)
    normed = widened / root_mean
    hidden = (normed * normalizer_scales).astype(jnp.bfloat16)
    middle_product = jnp.einsum(
        "qgr,vr->qgv",
        filtered_sensitivity_lines,
        lifting_projections,
        preferred_element_type=jnp.float32,
    )
    middle_product = jnp.where(column_mask, middle_product, 0.0).astype(jnp.bfloat16)
    weight_full, down_full = (
        lax.all_gather(frozen_projection_kernel, "fsdp", axis=0, tiled=True),
        lax.all_gather(lowering_projections, "fsdp", axis=0, tiled=True),
    )
    base_part = base_grad(filtered_sensitivity_lines, weight_full)
    projected = jnp.einsum("srd,dm->srm", hidden, down_full, preferred_element_type=jnp.float32)
    projected = jnp.where(column_mask, projected, 0.0).astype(jnp.bfloat16)
    hidden_grad = base_part.astype(jnp.float32) + jnp.einsum(
        "srm,dm->srd", middle_product, down_full, preferred_element_type=jnp.float32
    )
    scaled = hidden_grad * normalizer_scales
    residual_grad = (
        (scaled - normed * jnp.mean(scaled * normed, axis=-1, keepdims=True)) / root_mean
    ).astype(jnp.bfloat16)
    term_down = jnp.einsum(
        "srd,srm->dm", hidden, middle_product, preferred_element_type=jnp.float32
    )
    term_up = jnp.einsum(
        "srm,srk->mk", projected, filtered_sensitivity_lines, preferred_element_type=jnp.float32
    )
    sum_down, sum_up = (
        lax.psum_scatter(term_down, ("fsdp", "dp"), scatter_dimension=0, tiled=True),
        lax.psum_scatter(term_up, ("fsdp", "dp"), scatter_dimension=1, tiled=True),
    )
    inverse = jnp.repeat(1.0 / (BLOCK * block_count), LOW_DIM)
    return (residual_grad, sum_down * inverse[None, :], sum_up * inverse[:, None])


def nt_dot(a, b):
    return lax.dot_general(a, b, (((1,), (1,)), ((), ())), preferred_element_type=F32)


def tn_dot(a, b):
    return lax.dot_general(a, b, (((0,), (0,)), ((), ())), preferred_element_type=F32)


def cost(microseconds):
    return pl.CostEstimate(flops=int(microseconds * 1000), bytes_accessed=1000, transcendentals=0)


def params(mib=20):
    return pltpu.CompilerParams(vmem_limit_bytes=mib * MIB)


def member_mask(local, rows, shape, token_axis):
    slot = lax.broadcasted_iota(jnp.int32, shape, token_axis) // rows
    column_member = lax.broadcasted_iota(jnp.int32, shape, 1 - token_axis) // LOW_DIM
    token_member = jnp.full(shape, -1, jnp.int32)
    for s, e in enumerate(local):
        token_member = jnp.where(slot == s, e, token_member)
    return token_member == column_member


HBM = pl.BlockSpec(memory_space=pltpu.HBM)
VMEM = pl.BlockSpec(memory_space=pltpu.VMEM)
SMEM = pl.BlockSpec(memory_space=pltpu.SMEM)
ROWS = 128
COLUMNS = 256


class Copies:
    def __init__(self, sems):
        self.sems = sems
        self.used = 0

    def start(self, pairs):
        group = []
        for source, target in pairs:
            copy = pltpu.make_async_copy(source, target, self.sems.at[self.used])
            self.used += 1
            copy.start()
            group.append(copy)
        return group


def wait(group):
    for copy in group:
        copy.wait()


def quarters(width):
    step = width // 4
    return [slice(q * step, (q + 1) * step) for q in range(4)]


def norm_kernel(slot_ref, skip_ref, grad_ref, up_ref, inv_ref, mid_ref, turned_ref):
    tokens, width = skip_ref.shape
    low = up_ref.shape[0]
    count = slot_ref.shape[0]
    rows = tokens // count
    for first in range(0, tokens, ROWS):
        at = slice(first, first + ROWS)
        local = [slot_ref[s] for s in range(at.start // rows, at.stop // rows)]
        across = member_mask(local, rows, (ROWS, low), 0)
        along = member_mask(local, rows, (low, ROWS), 1)
        mid_ref[at, :] = jnp.where(across, nt_dot(grad_ref[at, :], up_ref[...]), 0.0).astype(BF16)
        turned_ref[:, at] = jnp.where(along, nt_dot(up_ref[...], grad_ref[at, :]), 0.0).astype(BF16)
        totals = [jnp.zeros((ROWS, 128), F32), jnp.zeros((ROWS, 128), F32)]
        for j in range(width // 128):
            wide = skip_ref[at, j * 128 : (j + 1) * 128].astype(F32)
            totals[j % 2] += wide * wide
        mean = jnp.sum(totals[0] + totals[1], axis=-1, keepdims=True) / width
        inv_ref[at, :] = jnp.broadcast_to(lax.rsqrt(mean + epsilon), (ROWS, 128))


def norm_call(slots_local, skip, grad, up):
    tokens, width = skip.shape
    low = up.shape[0]
    return pl.pallas_call(
        norm_kernel,
        out_shape=(
            pltpu.VMEM((tokens, 128), F32),
            pltpu.VMEM((tokens, low), BF16),
            pltpu.VMEM((low, tokens), BF16),
        ),
        in_specs=[SMEM, VMEM, VMEM, VMEM],
        out_specs=[VMEM] * 3,
        compiler_params=params(),
        cost_estimate=cost(2.5),
        name="norm",
    )(slots_local, skip, grad, up)


def terms_kernel(fsdp, slot_ref, place_ref, skip_ref, grad_ref, inv_ref, scale_ref, turned_ref, own_ref, *rest):
    far_refs, rest = rest[: 2 * (fsdp - 1)], rest[2 * (fsdp - 1) :]
    keep_out, send_out, term_ref, hidden_ref, down_ref, up_ref, sems = rest
    outs = (keep_out, send_out)
    core = place_ref[0]
    tokens, width = skip_ref.shape
    n = width // fsdp
    half = n // 2
    low = turned_ref.shape[0]
    copies = Copies(sems)
    inverse = inv_ref[...]
    projected = jnp.zeros((tokens, low), F32)
    stores = []
    for r in range(fsdp):
        start = lax.rem(place_ref[1] + r, fsdp) * n
        if r == 0:
            down = own_ref[...]
        else:
            for k in range(2):
                down_ref[core ^ k] = far_refs[k * (fsdp - 1) + r - 1][...]
            down = down_ref[...].reshape(n, low)
        for j in range(n // 128):
            cols = pl.ds(pl.multiple_of(start + j * 128, 128), 128)
            hidden_ref[r, :, j * 128 : (j + 1) * 128] = (skip_ref[:, cols].astype(F32) * inverse * scale_ref[:, cols]).astype(BF16)
        term = jnp.dot(turned_ref[...], hidden_ref[r], preferred_element_type=F32)
        for h in range(2):
            term_ref[core ^ h, r, :, :half] = term[:, h * half : (h + 1) * half]
        stores += copies.start([(term_ref.at[h, r, :, pl.ds(0, half)], outs[h].at[r, :, pl.ds(0, half)]) for h in range(2)])
        projected += jnp.dot(hidden_ref[r], down, preferred_element_type=F32)
    count = slot_ref.shape[0]
    mask = member_mask([slot_ref[s] for s in range(count)], tokens // count, (tokens, low), 0)
    projected = jnp.where(mask, projected, 0.0).astype(BF16)
    up_ref[...] = tn_dot(projected, grad_ref[...])
    for r in range(fsdp):
        shard = lax.rem(place_ref[1] + r, fsdp)
        for h in range(2):
            at = pl.multiple_of((shard * 2 + (core ^ h)) * 128, 128)
            term_ref[h, r, :, half:] = up_ref[:, pl.ds(at, 128)]
    stores += copies.start([(term_ref.at[h, :, :, pl.ds(half, 128)], outs[h].at[:, :, pl.ds(half, 128)]) for h in range(2)])
    wait(stores)


def terms_call(slots_local, place, skip, inv, scales, turned, down, keep, other, grad):
    tokens, width = skip.shape
    low = turned.shape[0]
    n = down.shape[0]
    fsdp = width // n
    both = n // 2 + 128
    out = jax.ShapeDtypeStruct((fsdp, low, both), F32)
    return pl.pallas_call(
        functools.partial(terms_kernel, fsdp),
        out_shape=(out, out),
        in_specs=[SMEM, SMEM] + [VMEM] * (6 + 2 * (fsdp - 1)),
        out_specs=[pl.BlockSpec(memory_space=pl.ANY)] * 2,
        scratch_shapes=[
            pltpu.VMEM((2, fsdp, low, both), F32),
            pltpu.VMEM((fsdp, tokens, n), BF16),
            pltpu.VMEM((2, n // 2, low), BF16),
            pltpu.VMEM((low, grad.shape[1]), F32),
            pltpu.SemaphoreType.DMA((2 * fsdp + 2,)),
        ],
        compiler_params=params(),
        cost_estimate=cost(7.5),
        name="terms",
    )(slots_local, place, skip, grad, inv, scales, turned, down, *keep, *other)


def base_kernel(r, fsdp, spans, place_ref, grad_ref, mid_ref, skip_ref, scale_ref, *rest):
    *ins, out_ref, sum_ref, both_ref, down_ref = rest
    tokens, n = out_ref.shape
    kdim = grad_ref.shape[1]
    core = place_ref[0]
    start = lax.rem(place_ref[1] + r, fsdp) * n
    half = n // 2
    if r:
        for j in range(kdim // 128):
            at = pl.multiple_of((place_ref[2] ^ j) * 128, 128)
            both_ref[:, j * 128 : (j + 1) * 128] = grad_ref[:, pl.ds(at, 128)]
        for k in range(2):
            at = pl.multiple_of((core ^ k) * half, half)
            down_ref[pl.ds(at, half), :] = ins[len(spans) + k][...]
    else:
        both_ref[:, :kdim] = grad_ref[...]
        down_ref[...] = ins[1][...]
    both_ref[:, kdim:] = mid_ref[...]
    total = jnp.zeros(sum_ref.shape, F32)
    for i in range(n // COLUMNS):
        rows = slice(i * COLUMNS, (i + 1) * COLUMNS)
        parts = [ref[first + rows.start : first + rows.stop, :] for ref, first in zip(ins, spans)]
        weight = jnp.concatenate(parts + [down_ref[rows, :]], axis=-1)
        scale = scale_ref[:, pl.ds(pl.multiple_of(start + i * COLUMNS, 128), COLUMNS)]
        scaled = nt_dot(both_ref[...], weight) * scale
        out_ref[:, rows] = scaled.astype(BF16)
        for j in range(COLUMNS // 128):
            cols = pl.ds(pl.multiple_of(start + i * COLUMNS + j * 128, 128), 128)
            total += scaled[:, j * 128 : (j + 1) * 128] * skip_ref[:, cols].astype(F32)
    sum_ref[...] = total


def base_call(r, fsdp, place, grad, mid, skip, scales, spans, ins):
    tokens, kdim = grad.shape
    low = mid.shape[1]
    n = skip.shape[1] // fsdp
    return pl.pallas_call(
        functools.partial(base_kernel, r, fsdp, spans),
        out_shape=(pltpu.VMEM((tokens, n), BF16), pltpu.VMEM((tokens, 128), F32)),
        in_specs=[SMEM] + [VMEM] * (4 + len(ins)),
        out_specs=[VMEM] * 2,
        scratch_shapes=[
            pltpu.VMEM((tokens, kdim + low), BF16),
            pltpu.VMEM((n, low), BF16),
        ],
        compiler_params=params(),
        cost_estimate=cost(3.4),
        name="base",
    )(place, grad, mid, skip, scales, *ins)


def residual_kernel(fsdp, slot_ref, place_ref, skip_ref, inv_ref, *rest):
    base_refs, sum_refs, rest = rest[:fsdp], rest[fsdp : 2 * fsdp], rest[2 * fsdp :]
    out_hbm, done_ref, out_ref, keep_ref, pull_ref, sems = rest
    tokens, width = skip_ref.shape
    n = width // fsdp
    rows = tokens // slot_ref.shape[0]
    copies = Copies(sems)
    inverse = inv_ref[...]
    total = sum_refs[0][...]
    for ref in sum_refs[1:]:
        total = total + ref[...]
    mean = jnp.sum(total, axis=-1, keepdims=True) * inverse / width
    pull_ref[...] = mean * inverse
    for s in range(slot_ref.shape[0]):
        local = slot_ref[s]
        alive = jnp.logical_and(local >= 0, local < place_ref[3])
        at = slice(s * rows, (s + 1) * rows)
        keep_ref[at, :] = inverse[at, :] * jnp.where(alive, 1.0, 0.0)
    done_ref[...] = jnp.zeros_like(done_ref)
    stores = []
    for first in range(0, tokens, ROWS):

        def some_rows(k, carry):
            at = pl.ds(pl.multiple_of(first + k * 32, 32), 32)
            for r in range(fsdp):
                start = lax.rem(place_ref[1] + r, fsdp) * n
                for j in range(n // 128):
                    cols = pl.ds(pl.multiple_of(start + j * 128, 128), 128)
                    wide = skip_ref[at, cols].astype(F32)
                    scaled = base_refs[r][at, j * 128 : (j + 1) * 128].astype(F32)
                    out_ref[at, cols] = ((scaled - wide * pull_ref[at, :]) * keep_ref[at, :]).astype(BF16)
            return carry

        lax.fori_loop(0, ROWS // 32, some_rows, 0)
        at = pl.ds(first, ROWS)
        stores += copies.start([(out_ref.at[at, q], out_hbm.at[at, q]) for q in quarters(width)])
    wait(stores)


def residual_call(slots_local, place, skip, inv, bases, sums):
    tokens, width = skip.shape
    fsdp = len(bases)
    small = pltpu.VMEM((tokens, 128), F32)
    return pl.pallas_call(
        functools.partial(residual_kernel, fsdp),
        out_shape=(jax.ShapeDtypeStruct(skip.shape, BF16), jax.ShapeDtypeStruct((8, 128), F32)),
        in_specs=[SMEM, SMEM] + [VMEM] * (2 + 2 * fsdp),
        out_specs=(HBM, VMEM),
        scratch_shapes=[
            pltpu.VMEM((tokens, width), BF16),
            small,
            small,
            pltpu.SemaphoreType.DMA((4 * (tokens // ROWS),)),
        ],
        compiler_params=params(),
        cost_estimate=cost(4.7),
        name="residual",
    )(slots_local, place, skip, inv, *bases, *sums)


def both_kernel(keep_ref, got_ref, *out_refs):
    for r, ref in enumerate(out_refs):
        ref[...] = (keep_ref[r] + got_ref[r]).astype(ref.dtype)


def both_call(keep, got):
    fsdp, low, both = keep.shape
    held = jax.ShapeDtypeStruct((low, both), F32)
    return pl.pallas_call(
        both_kernel,
        out_shape=(held,) * (fsdp - 1) + (jax.ShapeDtypeStruct((low, both), BF16),),
        in_specs=[VMEM] * 2,
        out_specs=[VMEM] * fsdp,
        compiler_params=params(),
        cost_estimate=cost(0.4),
        name="both",
    )(keep, got)


def add_kernel(held_ref, got_ref, out_ref):
    out_ref[...] = (held_ref[...] + got_ref[...].astype(F32)).astype(BF16)


def add_call(held, got):
    return pl.pallas_call(
        add_kernel,
        out_shape=jax.ShapeDtypeStruct(held.shape, BF16),
        in_specs=[VMEM] * 2,
        out_specs=VMEM,
        compiler_params=params(),
        cost_estimate=cost(0.4),
        name="add",
    )(held, got)


def finish_kernel(slot_ref, held_ref, got_ref, done_ref, down_ref, up_ref):
    del done_ref
    total = held_ref[...] + got_ref[...].astype(F32)
    low = total.shape[0]
    member = lax.broadcasted_iota(jnp.int32, (low, 128), 0) // LOW_DIM
    counts = jnp.zeros((low, 128), F32)
    for s in range(slot_ref.shape[0]):
        counts += jnp.where(member == slot_ref[s], 1.0, 0.0)
    inverse = 1.0 / (BLOCK * counts)
    half = down_ref.shape[0]
    for j in range(half // 128):
        cols = slice(j * 128, (j + 1) * 128)
        down_ref[cols, :] = (total[:, cols] * inverse).T
    up_ref[...] = total[:, half:] * inverse


def finish_call(slots_local, held, got, done):
    low, both = held.shape
    half = both - 128
    return pl.pallas_call(
        finish_kernel,
        out_shape=(jax.ShapeDtypeStruct((half, low), F32), jax.ShapeDtypeStruct((low, 128), F32)),
        in_specs=[SMEM] + [VMEM] * 3,
        out_specs=[VMEM] * 2,
        compiler_params=params(),
        cost_estimate=cost(1.5),
        name="finish",
    )(slots_local, held, got, done)


SWAP = [(0, 1), (1, 0)]


def after(value, *deps):
    return lax.optimization_barrier((value, *deps))[0]


def per_device_square(
    fsdp,
    skip_stream,
    grad_stream,
    weight,
    down,
    up,
    scales,
    assignee,
):
    z = lax.axis_index("fsdp")
    c = lax.axis_index("dp")
    m = lax.axis_index("member")
    piece = c * 4 + lax.axis_index("parts") * 2 + m
    half = down.shape[0] // 2
    low = up.shape[0]
    members = low // LOW_DIM
    skip = skip_stream.reshape(-1, skip_stream.shape[2])
    grad = grad_stream.reshape(-1, grad_stream.shape[2])
    scale_row = scales[None, :]
    local = assignee - m * members
    place = jnp.stack([c, z, piece, jnp.int32(members)])

    shift = lambda v, r: lax.ppermute(v, "fsdp", [(i, (i + r) % fsdp) for i in range(fsdp)])
    over = lambda v, axis: lax.ppermute(v, axis, SWAP)
    gate = lax.optimization_barrier
    n = down.shape[0]

    def base(r, spans, ins):
        return base_call(r, fsdp, place, grad, mid, skip, scale_row, spans, ins)

    def core(value):
        return over(value, "dp")

    unit = lax.dynamic_slice_in_dim(weight, piece * 128, 128, 1)
    down_half = lax.dynamic_slice_in_dim(down, c * half, half, 0)
    u1, u3 = shift(unit, -1), shift(unit, 1)
    inv, mid, turned = norm_call(local, skip, grad, up)
    u1, u3, down_half, inv, mid, turned = gate((u1, u3, down_half, inv, mid, turned))

    u = jnp.concatenate([u1, u3], axis=0)
    x, y = over(u, "member"), over(u, "parts")
    keep = [shift(down_half, -r) for r in range(1, fsdp)]
    base0, sum0 = base(0, (0,), (weight, down))
    u, x, y, keep, u3, sum0 = gate((u, x, y, keep, u3, sum0))

    u2 = shift(u3, 1)
    d1, d3 = over(x[:n], "parts"), over(y[n:], "member")
    other = [core(v) for v in keep]
    far_u, far_x, far_y = core(u), core(x), core(y)
    turned, far_u, far_x, far_y = gate((turned, far_u, far_x, far_y))
    terms = terms_call(local, place, skip, inv, scale_row, turned, down, keep, other, grad)
    d1, d3, far_u, far_x, far_y, terms, u2 = gate((d1, d3, far_u, far_x, far_y, terms, u2))

    *held, sent = both_call(terms[0], core(terms[1]))
    x2, y2 = over(u2, "member"), over(u2, "parts")
    got = shift(sent, 1)
    base1, sum1 = base(1, (0, 0, 0, 0) * 2, (u, x, y, d1, far_u, far_x, far_y, core(d1), keep[0], other[0]))
    u2, x2, y2, d3, got, sum1 = gate((u2, x2, y2, d3, got, sum1))

    d2 = over(x2, "parts")
    got = shift(add_call(held[2], got), 1)
    far2 = [core(v) for v in (u2, x2, y2)]
    base3, sum3 = base(3, (n, n, n, 0) * 2, (u, x, y, d3, far_u, far_x, far_y, core(d3), keep[2], other[2]))
    d2, far2, sum3 = gate((d2, far2, sum3))

    got = shift(add_call(held[1], got), 1)
    base2, sum2 = base(2, (0,) * 8, (u2, x2, y2, d2, *far2, core(d2), keep[1], other[1]))
    residual, done = residual_call(local, place, skip, inv, (base0, base1, base2, base3), (sum0, sum1, sum2, sum3))
    grad_down, grad_up = finish_call(local, held[0], got, done)
    return residual.reshape(skip_stream.shape), grad_down, grad_up


def solution(mesh):
    placed = (
        P(("parts", "member"), ("fsdp", "dp"), None),
        P(("parts", "member"), ("fsdp", "dp"), None),
        P("fsdp", None),
        P("fsdp", ("parts", "member")),
        P(("parts", "member"), None),
        P(),
        P(("parts", "member")),
    )
    sizes = dict(mesh.shape)
    square = sizes["parts"] == 2 and sizes["member"] == 2 and sizes["dp"] == 2 and sizes["fsdp"] == 4
    return jax.shard_map(
        functools.partial(per_device_square, sizes["fsdp"]) if square else per_device_any,
        mesh=mesh,
        in_specs=placed,
        out_specs=(
            P(("parts", "member"), ("fsdp", "dp"), None),
            P(("fsdp", "dp"), ("parts", "member")),
            P(("parts", "member"), ("fsdp", "dp")),
        ),
        check_vma=False,
    )
```

```python
import functools

import jax
import jax.numpy as jnp
from jax import lax
from jax.experimental import pallas as pl
from jax.experimental.pallas import tpu as pltpu
from jax.sharding import PartitionSpec as P

LOW_DIM = 64
BLOCK = 512


epsilon = 1e-06

F32 = jnp.float32
BF16 = jnp.bfloat16
MIB = 1024 * 1024


def base_grad(grads, weight_rows):
    product = jnp.einsum("srk,nk->srn", grads, weight_rows, preferred_element_type=jnp.float32)
    return product.astype(jnp.bfloat16)


def per_device_any(
    skip_stream,
    projected_output_adjoint,
    frozen_projection_kernel,
    lowering_projections,
    lifting_projections,
    normalizer_scales,
    tile_assignee,
):
    within_group_indices = lifting_projections.shape[0] // LOW_DIM
    first_member = lax.axis_index("member") * within_group_indices
    member_ids = first_member + jnp.arange(within_group_indices, dtype=jnp.int32)
    onehot = tile_assignee[:, None] == member_ids[None, :]
    live_mask = jnp.any(onehot, axis=1)
    block_count = jnp.sum(onehot.astype(jnp.float32), axis=0)
    filtered_sensitivity_lines = jnp.where(
        live_mask[:, None, None], projected_output_adjoint, jnp.zeros_like(projected_output_adjoint)
    )
    column_mask = jnp.repeat(onehot, LOW_DIM, axis=1)[:, None, :]
    widened = skip_stream.astype(jnp.float32)
    root_mean = jnp.sqrt(jnp.mean(widened * widened, axis=-1, keepdims=True) + epsilon)
    normed = widened / root_mean
    hidden = (normed * normalizer_scales).astype(jnp.bfloat16)
    middle_product = jnp.einsum(
        "qgr,vr->qgv",
        filtered_sensitivity_lines,
        lifting_projections,
        preferred_element_type=jnp.float32,
    )
    middle_product = jnp.where(column_mask, middle_product, 0.0).astype(jnp.bfloat16)
    weight_full, down_full = (
        lax.all_gather(frozen_projection_kernel, "fsdp", axis=0, tiled=True),
        lax.all_gather(lowering_projections, "fsdp", axis=0, tiled=True),
    )
    base_part = base_grad(filtered_sensitivity_lines, weight_full)
    projected = jnp.einsum("srd,dm->srm", hidden, down_full, preferred_element_type=jnp.float32)
    projected = jnp.where(column_mask, projected, 0.0).astype(jnp.bfloat16)
    hidden_grad = base_part.astype(jnp.float32) + jnp.einsum(
        "srm,dm->srd", middle_product, down_full, preferred_element_type=jnp.float32
    )
    scaled = hidden_grad * normalizer_scales
    residual_grad = (
        (scaled - normed * jnp.mean(scaled * normed, axis=-1, keepdims=True)) / root_mean
    ).astype(jnp.bfloat16)
    term_down = jnp.einsum(
        "srd,srm->dm", hidden, middle_product, preferred_element_type=jnp.float32
    )
    term_up = jnp.einsum(
        "srm,srk->mk", projected, filtered_sensitivity_lines, preferred_element_type=jnp.float32
    )
    sum_down, sum_up = (
        lax.psum_scatter(term_down, ("fsdp", "dp"), scatter_dimension=0, tiled=True),
        lax.psum_scatter(term_up, ("fsdp", "dp"), scatter_dimension=1, tiled=True),
    )
    inverse = jnp.repeat(1.0 / (BLOCK * block_count), LOW_DIM)
    return (residual_grad, sum_down * inverse[None, :], sum_up * inverse[:, None])


def nt_dot(a, b):
    return lax.dot_general(a, b, (((1,), (1,)), ((), ())), preferred_element_type=F32)


def tn_dot(a, b):
    return lax.dot_general(a, b, (((0,), (0,)), ((), ())), preferred_element_type=F32)


def cost(microseconds):
    return pl.CostEstimate(flops=int(microseconds * 1000), bytes_accessed=1000, transcendentals=0)


def params(mib=20):
    return pltpu.CompilerParams(vmem_limit_bytes=mib * MIB)


def member_mask(local, rows, shape, token_axis):
    slot = lax.broadcasted_iota(jnp.int32, shape, token_axis) // rows
    column_member = lax.broadcasted_iota(jnp.int32, shape, 1 - token_axis) // LOW_DIM
    token_member = jnp.full(shape, -1, jnp.int32)
    for s, e in enumerate(local):
        token_member = jnp.where(slot == s, e, token_member)
    return token_member == column_member


HBM = pl.BlockSpec(memory_space=pltpu.HBM)
VMEM = pl.BlockSpec(memory_space=pltpu.VMEM)
SMEM = pl.BlockSpec(memory_space=pltpu.SMEM)
ROWS = 128
COLUMNS = 256


class Copies:
    def __init__(self, sems):
        self.sems = sems
        self.used = 0

    def start(self, pairs):
        group = []
        for source, target in pairs:
            copy = pltpu.make_async_copy(source, target, self.sems.at[self.used])
            self.used += 1
            copy.start()
            group.append(copy)
        return group


def wait(group):
    for copy in group:
        copy.wait()


def quarters(width):
    step = width // 4
    return [slice(q * step, (q + 1) * step) for q in range(4)]


def norm_kernel(slot_ref, skip_ref, grad_ref, up_ref, inv_ref, mid_ref, turned_ref):
    tokens, width = skip_ref.shape
    low = up_ref.shape[0]
    count = slot_ref.shape[0]
    rows = tokens // count
    for first in range(0, tokens, ROWS):
        at = slice(first, first + ROWS)
        local = [slot_ref[s] for s in range(at.start // rows, at.stop // rows)]
        across = member_mask(local, rows, (ROWS, low), 0)
        along = member_mask(local, rows, (low, ROWS), 1)
        mid_ref[at, :] = jnp.where(across, nt_dot(grad_ref[at, :], up_ref[...]), 0.0).astype(BF16)
        turned_ref[:, at] = jnp.where(along, nt_dot(up_ref[...], grad_ref[at, :]), 0.0).astype(BF16)
        totals = [jnp.zeros((ROWS, 128), F32), jnp.zeros((ROWS, 128), F32)]
        for j in range(width // 128):
            wide = skip_ref[at, j * 128 : (j + 1) * 128].astype(F32)
            totals[j % 2] += wide * wide
        mean = jnp.sum(totals[0] + totals[1], axis=-1, keepdims=True) / width
        inv_ref[at, :] = jnp.broadcast_to(lax.rsqrt(mean + epsilon), (ROWS, 128))


def norm_call(slots_local, skip, grad, up):
    tokens, width = skip.shape
    low = up.shape[0]
    return pl.pallas_call(
        norm_kernel,
        out_shape=(
            pltpu.VMEM((tokens, 128), F32),
            pltpu.VMEM((tokens, low), BF16),
            pltpu.VMEM((low, tokens), BF16),
        ),
        in_specs=[SMEM, VMEM, VMEM, VMEM],
        out_specs=[VMEM] * 3,
        compiler_params=params(),
        cost_estimate=cost(2.5),
        name="norm",
    )(slots_local, skip, grad, up)


def terms_kernel(fsdp, slot_ref, place_ref, skip_ref, grad_ref, inv_ref, scale_ref, turned_ref, own_ref, *rest):
    far_refs, rest = rest[: 2 * (fsdp - 1)], rest[2 * (fsdp - 1) :]
    keep_out, send_out, hidden_ref, down_ref, up_ref = rest
    outs = (keep_out, send_out)
    core = place_ref[0]
    tokens, width = skip_ref.shape
    n = width // fsdp
    half = n // 2
    low = turned_ref.shape[0]
    first = core == 0
    inverse = inv_ref[...]
    projected = jnp.zeros((tokens, low), F32)
    for r in range(fsdp):
        start = lax.rem(place_ref[1] + r, fsdp) * n
        if r == 0:
            down = own_ref[...]
        else:
            mine, theirs = far_refs[r - 1][...], far_refs[fsdp - 1 + r - 1][...]
            down_ref[:half, :] = jnp.where(first, mine, theirs)
            down_ref[half:, :] = jnp.where(first, theirs, mine)
            down = down_ref[...]
        for j in range(n // 128):
            cols = pl.ds(pl.multiple_of(start + j * 128, 128), 128)
            hidden_ref[r, :, j * 128 : (j + 1) * 128] = (skip_ref[:, cols].astype(F32) * inverse * scale_ref[:, cols]).astype(BF16)
        term = jnp.dot(turned_ref[...], hidden_ref[r], preferred_element_type=F32)
        low_half, high_half = term[:, :half], term[:, half:]
        keep_out[r, :, :half] = jnp.where(first, low_half, high_half)
        send_out[r, :, :half] = jnp.where(first, high_half, low_half)
        projected += jnp.dot(hidden_ref[r], down, preferred_element_type=F32)
    count = slot_ref.shape[0]
    mask = member_mask([slot_ref[s] for s in range(count)], tokens // count, (tokens, low), 0)
    projected = jnp.where(mask, projected, 0.0).astype(BF16)
    up_ref[...] = tn_dot(projected, grad_ref[...])
    for r in range(fsdp):
        shard = lax.rem(place_ref[1] + r, fsdp)
        for h in range(2):
            at = pl.multiple_of((shard * 2 + (core ^ h)) * 128, 128)
            outs[h][r, :, half:] = up_ref[:, pl.ds(at, 128)]


def terms_call(slots_local, place, skip, inv, scales, turned, down, keep, other, grad):
    tokens, width = skip.shape
    low = turned.shape[0]
    n = down.shape[0]
    fsdp = width // n
    both = n // 2 + 128
    out = jax.ShapeDtypeStruct((fsdp, low, both), F32)
    return pl.pallas_call(
        functools.partial(terms_kernel, fsdp),
        out_shape=(out, out),
        in_specs=[SMEM, SMEM] + [VMEM] * (6 + 2 * (fsdp - 1)),
        out_specs=[VMEM] * 2,
        scratch_shapes=[
            pltpu.VMEM((fsdp, tokens, n), BF16),
            pltpu.VMEM((n, low), BF16),
            pltpu.VMEM((low, grad.shape[1]), F32),
        ],
        compiler_params=params(),
        cost_estimate=cost(7.5),
        name="terms",
    )(slots_local, place, skip, grad, inv, scales, turned, down, *keep, *other)


def base_kernel(r, fsdp, spans, place_ref, grad_ref, mid_ref, skip_ref, scale_ref, *rest):
    *ins, out_ref, sum_ref, both_ref, down_ref = rest
    tokens, n = out_ref.shape
    kdim = grad_ref.shape[1]
    core = place_ref[0]
    start = lax.rem(place_ref[1] + r, fsdp) * n
    half = n // 2
    if r:
        for j in range(kdim // 128):
            at = pl.multiple_of((place_ref[2] ^ j) * 128, 128)
            both_ref[:, j * 128 : (j + 1) * 128] = grad_ref[:, pl.ds(at, 128)]
        for k in range(2):
            at = pl.multiple_of((core ^ k) * half, half)
            down_ref[pl.ds(at, half), :] = ins[len(spans) + k][...]
    else:
        both_ref[:, :kdim] = grad_ref[...]
        down_ref[...] = ins[1][...]
    both_ref[:, kdim:] = mid_ref[...]
    total = jnp.zeros(sum_ref.shape, F32)
    for i in range(n // COLUMNS):
        rows = slice(i * COLUMNS, (i + 1) * COLUMNS)
        parts = [ref[first + rows.start : first + rows.stop, :] for ref, first in zip(ins, spans)]
        weight = jnp.concatenate(parts + [down_ref[rows, :]], axis=-1)
        scale = scale_ref[:, pl.ds(pl.multiple_of(start + i * COLUMNS, 128), COLUMNS)]
        scaled = nt_dot(both_ref[...], weight) * scale
        out_ref[:, rows] = scaled.astype(BF16)
        for j in range(COLUMNS // 128):
            cols = pl.ds(pl.multiple_of(start + i * COLUMNS + j * 128, 128), 128)
            total += scaled[:, j * 128 : (j + 1) * 128] * skip_ref[:, cols].astype(F32)
    sum_ref[...] = total


def base_call(r, fsdp, place, grad, mid, skip, scales, spans, ins):
    tokens, kdim = grad.shape
    low = mid.shape[1]
    n = skip.shape[1] // fsdp
    return pl.pallas_call(
        functools.partial(base_kernel, r, fsdp, spans),
        out_shape=(pltpu.VMEM((tokens, n), BF16), pltpu.VMEM((tokens, 128), F32)),
        in_specs=[SMEM] + [VMEM] * (4 + len(ins)),
        out_specs=[VMEM] * 2,
        scratch_shapes=[
            pltpu.VMEM((tokens, kdim + low), BF16),
            pltpu.VMEM((n, low), BF16),
        ],
        compiler_params=params(),
        cost_estimate=cost(3.4),
        name="base",
    )(place, grad, mid, skip, scales, *ins)


def residual_kernel(fsdp, slot_ref, place_ref, skip_ref, inv_ref, *rest):
    base_refs, sum_refs, rest = rest[:fsdp], rest[fsdp : 2 * fsdp], rest[2 * fsdp :]
    out_hbm, done_ref, out_ref, keep_ref, pull_ref, sems = rest
    tokens, width = skip_ref.shape
    n = width // fsdp
    rows = tokens // slot_ref.shape[0]
    copies = Copies(sems)
    inverse = inv_ref[...]
    total = sum_refs[0][...]
    for ref in sum_refs[1:]:
        total = total + ref[...]
    mean = jnp.sum(total, axis=-1, keepdims=True) * inverse / width
    pull_ref[...] = mean * inverse
    for s in range(slot_ref.shape[0]):
        local = slot_ref[s]
        alive = jnp.logical_and(local >= 0, local < place_ref[3])
        at = slice(s * rows, (s + 1) * rows)
        keep_ref[at, :] = inverse[at, :] * jnp.where(alive, 1.0, 0.0)
    done_ref[...] = jnp.zeros_like(done_ref)
    stores = []
    for first in range(0, tokens, ROWS):

        def some_rows(k, carry):
            at = pl.ds(pl.multiple_of(first + k * 32, 32), 32)
            for r in range(fsdp):
                start = lax.rem(place_ref[1] + r, fsdp) * n
                for j in range(n // 128):
                    cols = pl.ds(pl.multiple_of(start + j * 128, 128), 128)
                    wide = skip_ref[at, cols].astype(F32)
                    scaled = base_refs[r][at, j * 128 : (j + 1) * 128].astype(F32)
                    out_ref[at, cols] = ((scaled - wide * pull_ref[at, :]) * keep_ref[at, :]).astype(BF16)
            return carry

        lax.fori_loop(0, ROWS // 32, some_rows, 0)
        at = pl.ds(first, ROWS)
        stores += copies.start([(out_ref.at[at, q], out_hbm.at[at, q]) for q in quarters(width)])
    wait(stores)


def residual_call(slots_local, place, skip, inv, bases, sums):
    tokens, width = skip.shape
    fsdp = len(bases)
    small = pltpu.VMEM((tokens, 128), F32)
    return pl.pallas_call(
        functools.partial(residual_kernel, fsdp),
        out_shape=(jax.ShapeDtypeStruct(skip.shape, BF16), jax.ShapeDtypeStruct((8, 128), F32)),
        in_specs=[SMEM, SMEM] + [VMEM] * (2 + 2 * fsdp),
        out_specs=(HBM, VMEM),
        scratch_shapes=[
            pltpu.VMEM((tokens, width), BF16),
            small,
            small,
            pltpu.SemaphoreType.DMA((4 * (tokens // ROWS),)),
        ],
        compiler_params=params(),
        cost_estimate=cost(4.7),
        name="residual",
    )(slots_local, place, skip, inv, *bases, *sums)


def both_kernel(keep_ref, got_ref, *out_refs):
    for r, ref in enumerate(out_refs):
        ref[...] = (keep_ref[r] + got_ref[r]).astype(ref.dtype)


def both_call(keep, got):
    fsdp, low, both = keep.shape
    held = jax.ShapeDtypeStruct((low, both), F32)
    return pl.pallas_call(
        both_kernel,
        out_shape=(held,) * (fsdp - 1) + (jax.ShapeDtypeStruct((low, both), BF16),),
        in_specs=[VMEM] * 2,
        out_specs=[VMEM] * fsdp,
        compiler_params=params(),
        cost_estimate=cost(0.4),
        name="both",
    )(keep, got)


def add_kernel(held_ref, got_ref, out_ref):
    out_ref[...] = (held_ref[...] + got_ref[...].astype(F32)).astype(BF16)


def add_call(held, got):
    return pl.pallas_call(
        add_kernel,
        out_shape=jax.ShapeDtypeStruct(held.shape, BF16),
        in_specs=[VMEM] * 2,
        out_specs=VMEM,
        compiler_params=params(),
        cost_estimate=cost(0.4),
        name="add",
    )(held, got)


def finish_kernel(slot_ref, held_ref, got_ref, done_ref, down_ref, up_ref):
    del done_ref
    total = held_ref[...] + got_ref[...].astype(F32)
    low = total.shape[0]
    member = lax.broadcasted_iota(jnp.int32, (low, 128), 0) // LOW_DIM
    counts = jnp.zeros((low, 128), F32)
    for s in range(slot_ref.shape[0]):
        counts += jnp.where(member == slot_ref[s], 1.0, 0.0)
    inverse = 1.0 / (BLOCK * counts)
    half = down_ref.shape[0]
    for j in range(half // 128):
        cols = slice(j * 128, (j + 1) * 128)
        down_ref[cols, :] = (total[:, cols] * inverse).T
    up_ref[...] = total[:, half:] * inverse


def finish_call(slots_local, held, got, done):
    low, both = held.shape
    half = both - 128
    return pl.pallas_call(
        finish_kernel,
        out_shape=(jax.ShapeDtypeStruct((half, low), F32), jax.ShapeDtypeStruct((low, 128), F32)),
        in_specs=[SMEM] + [VMEM] * 3,
        out_specs=[VMEM] * 2,
        compiler_params=params(),
        cost_estimate=cost(1.5),
        name="finish",
    )(slots_local, held, got, done)


SWAP = [(0, 1), (1, 0)]


def after(value, *deps):
    return lax.optimization_barrier((value, *deps))[0]


def per_device_square(
    fsdp,
    skip_stream,
    grad_stream,
    weight,
    down,
    up,
    scales,
    assignee,
):
    z = lax.axis_index("fsdp")
    c = lax.axis_index("dp")
    m = lax.axis_index("member")
    piece = c * 4 + lax.axis_index("parts") * 2 + m
    half = down.shape[0] // 2
    low = up.shape[0]
    members = low // LOW_DIM
    skip = skip_stream.reshape(-1, skip_stream.shape[2])
    grad = grad_stream.reshape(-1, grad_stream.shape[2])
    scale_row = scales[None, :]
    local = assignee - m * members
    place = jnp.stack([c, z, piece, jnp.int32(members)])

    shift = lambda v, r: lax.ppermute(v, "fsdp", [(i, (i + r) % fsdp) for i in range(fsdp)])
    over = lambda v, axis: lax.ppermute(v, axis, SWAP)
    gate = lax.optimization_barrier
    n = down.shape[0]

    def base(r, spans, ins):
        return base_call(r, fsdp, place, grad, mid, skip, scale_row, spans, ins)

    def core(value):
        return over(value, "dp")

    unit = lax.dynamic_slice_in_dim(weight, piece * 128, 128, 1)
    down_half = lax.dynamic_slice_in_dim(down, c * half, half, 0)
    u1, u3 = shift(unit, -1), shift(unit, 1)
    inv, mid, turned = norm_call(local, skip, grad, up)
    u1, u3, down_half, inv, mid, turned = gate((u1, u3, down_half, inv, mid, turned))

    u = jnp.concatenate([u1, u3], axis=0)
    x, y = over(u, "member"), over(u, "parts")
    keep = [shift(down_half, -r) for r in range(1, fsdp)]
    base0, sum0 = base(0, (0,), (weight, down))
    u, x, y, keep, u3, sum0 = gate((u, x, y, keep, u3, sum0))

    u2 = shift(u3, 1)
    d1, d3 = over(x[:n], "parts"), over(y[n:], "member")
    other = [core(v) for v in keep]
    far_u, far_x, far_y = core(u), core(x), core(y)
    turned, far_u, far_x, far_y = gate((turned, far_u, far_x, far_y))
    terms = terms_call(local, place, skip, inv, scale_row, turned, down, keep, other, grad)
    d1, d3, far_u, far_x, far_y, terms, u2 = gate((d1, d3, far_u, far_x, far_y, terms, u2))

    *held, sent = both_call(terms[0], core(terms[1]))
    x2, y2 = over(u2, "member"), over(u2, "parts")
    got = shift(sent, 1)
    base1, sum1 = base(1, (0, 0, 0, 0) * 2, (u, x, y, d1, far_u, far_x, far_y, core(d1), keep[0], other[0]))
    u2, x2, y2, d3, got, sum1 = gate((u2, x2, y2, d3, got, sum1))

    d2 = over(x2, "parts")
    got = shift(add_call(held[2], got), 1)
    far2 = [core(v) for v in (u2, x2, y2)]
    base3, sum3 = base(3, (n, n, n, 0) * 2, (u, x, y, d3, far_u, far_x, far_y, core(d3), keep[2], other[2]))
    d2, far2, sum3 = gate((d2, far2, sum3))

    got = shift(add_call(held[1], got), 1)
    base2, sum2 = base(2, (0,) * 8, (u2, x2, y2, d2, *far2, core(d2), keep[1], other[1]))
    residual, done = residual_call(local, place, skip, inv, (base0, base1, base2, base3), (sum0, sum1, sum2, sum3))
    grad_down, grad_up = finish_call(local, held[0], got, done)
    return residual.reshape(skip_stream.shape), grad_down, grad_up


def solution(mesh):
    placed = (
        P(("parts", "member"), ("fsdp", "dp"), None),
        P(("parts", "member"), ("fsdp", "dp"), None),
        P("fsdp", None),
        P("fsdp", ("parts", "member")),
        P(("parts", "member"), None),
        P(),
        P(("parts", "member")),
    )
    sizes = dict(mesh.shape)
    square = sizes["parts"] == 2 and sizes["member"] == 2 and sizes["dp"] == 2 and sizes["fsdp"] == 4
    return jax.shard_map(
        functools.partial(per_device_square, sizes["fsdp"]) if square else per_device_any,
        mesh=mesh,
        in_specs=placed,
        out_specs=(
            P(("parts", "member"), ("fsdp", "dp"), None),
            P(("fsdp", "dp"), ("parts", "member")),
            P(("parts", "member"), ("fsdp", "dp")),
        ),
        check_vma=False,
    )
```

```python
import functools

import jax
import jax.numpy as jnp
from jax import lax
from jax.experimental import pallas as pl
from jax.experimental.pallas import tpu as pltpu
from jax.sharding import PartitionSpec as P

LOW_DIM = 64
BLOCK = 512


epsilon = 1e-06

F32 = jnp.float32
BF16 = jnp.bfloat16
MIB = 1024 * 1024


def base_grad(grads, weight_rows):
    product = jnp.einsum("srk,nk->srn", grads, weight_rows, preferred_element_type=jnp.float32)
    return product.astype(jnp.bfloat16)


def per_device_any(
    skip_stream,
    projected_output_adjoint,
    frozen_projection_kernel,
    lowering_projections,
    lifting_projections,
    normalizer_scales,
    tile_assignee,
):
    within_group_indices = lifting_projections.shape[0] // LOW_DIM
    first_member = lax.axis_index("member") * within_group_indices
    member_ids = first_member + jnp.arange(within_group_indices, dtype=jnp.int32)
    onehot = tile_assignee[:, None] == member_ids[None, :]
    live_mask = jnp.any(onehot, axis=1)
    block_count = jnp.sum(onehot.astype(jnp.float32), axis=0)
    filtered_sensitivity_lines = jnp.where(
        live_mask[:, None, None], projected_output_adjoint, jnp.zeros_like(projected_output_adjoint)
    )
    column_mask = jnp.repeat(onehot, LOW_DIM, axis=1)[:, None, :]
    widened = skip_stream.astype(jnp.float32)
    root_mean = jnp.sqrt(jnp.mean(widened * widened, axis=-1, keepdims=True) + epsilon)
    normed = widened / root_mean
    hidden = (normed * normalizer_scales).astype(jnp.bfloat16)
    middle_product = jnp.einsum(
        "qgr,vr->qgv",
        filtered_sensitivity_lines,
        lifting_projections,
        preferred_element_type=jnp.float32,
    )
    middle_product = jnp.where(column_mask, middle_product, 0.0).astype(jnp.bfloat16)
    weight_full, down_full = (
        lax.all_gather(frozen_projection_kernel, "fsdp", axis=0, tiled=True),
        lax.all_gather(lowering_projections, "fsdp", axis=0, tiled=True),
    )
    base_part = base_grad(filtered_sensitivity_lines, weight_full)
    projected = jnp.einsum("srd,dm->srm", hidden, down_full, preferred_element_type=jnp.float32)
    projected = jnp.where(column_mask, projected, 0.0).astype(jnp.bfloat16)
    hidden_grad = base_part.astype(jnp.float32) + jnp.einsum(
        "srm,dm->srd", middle_product, down_full, preferred_element_type=jnp.float32
    )
    scaled = hidden_grad * normalizer_scales
    residual_grad = (
        (scaled - normed * jnp.mean(scaled * normed, axis=-1, keepdims=True)) / root_mean
    ).astype(jnp.bfloat16)
    term_down = jnp.einsum(
        "srd,srm->dm", hidden, middle_product, preferred_element_type=jnp.float32
    )
    term_up = jnp.einsum(
        "srm,srk->mk", projected, filtered_sensitivity_lines, preferred_element_type=jnp.float32
    )
    sum_down, sum_up = (
        lax.psum_scatter(term_down, ("fsdp", "dp"), scatter_dimension=0, tiled=True),
        lax.psum_scatter(term_up, ("fsdp", "dp"), scatter_dimension=1, tiled=True),
    )
    inverse = jnp.repeat(1.0 / (BLOCK * block_count), LOW_DIM)
    return (residual_grad, sum_down * inverse[None, :], sum_up * inverse[:, None])


def nt_dot(a, b):
    return lax.dot_general(a, b, (((1,), (1,)), ((), ())), preferred_element_type=F32)


def tn_dot(a, b):
    return lax.dot_general(a, b, (((0,), (0,)), ((), ())), preferred_element_type=F32)


def cost(microseconds):
    return pl.CostEstimate(flops=int(microseconds * 1000), bytes_accessed=1000, transcendentals=0)


def params(mib=20):
    return pltpu.CompilerParams(vmem_limit_bytes=mib * MIB)


def member_mask(local, rows, shape, token_axis):
    slot = lax.broadcasted_iota(jnp.int32, shape, token_axis) // rows
    column_member = lax.broadcasted_iota(jnp.int32, shape, 1 - token_axis) // LOW_DIM
    token_member = jnp.full(shape, -1, jnp.int32)
    for s, e in enumerate(local):
        token_member = jnp.where(slot == s, e, token_member)
    return token_member == column_member


HBM = pl.BlockSpec(memory_space=pltpu.HBM)
VMEM = pl.BlockSpec(memory_space=pltpu.VMEM)
SMEM = pl.BlockSpec(memory_space=pltpu.SMEM)
ROWS = 128
COLUMNS = 256


class Copies:
    def __init__(self, sems):
        self.sems = sems
        self.used = 0

    def start(self, pairs):
        group = []
        for source, target in pairs:
            copy = pltpu.make_async_copy(source, target, self.sems.at[self.used])
            self.used += 1
            copy.start()
            group.append(copy)
        return group


def wait(group):
    for copy in group:
        copy.wait()


def quarters(width):
    step = width // 4
    return [slice(q * step, (q + 1) * step) for q in range(4)]


def norm_kernel(slot_ref, skip_ref, grad_ref, up_ref, inv_ref, mid_ref, turned_ref):
    tokens, width = skip_ref.shape
    low = up_ref.shape[0]
    count = slot_ref.shape[0]
    rows = tokens // count
    for first in range(0, tokens, ROWS):
        at = slice(first, first + ROWS)
        local = [slot_ref[s] for s in range(at.start // rows, at.stop // rows)]
        across = member_mask(local, rows, (ROWS, low), 0)
        along = member_mask(local, rows, (low, ROWS), 1)
        mid_ref[at, :] = jnp.where(across, nt_dot(grad_ref[at, :], up_ref[...]), 0.0).astype(BF16)
        turned_ref[:, at] = jnp.where(along, nt_dot(up_ref[...], grad_ref[at, :]), 0.0).astype(BF16)
        totals = [jnp.zeros((ROWS, 128), F32), jnp.zeros((ROWS, 128), F32)]
        for j in range(width // 128):
            wide = skip_ref[at, j * 128 : (j + 1) * 128].astype(F32)
            totals[j % 2] += wide * wide
        mean = jnp.sum(totals[0] + totals[1], axis=-1, keepdims=True) / width
        inv_ref[at, :] = jnp.broadcast_to(lax.rsqrt(mean + epsilon), (ROWS, 128))


def norm_call(slots_local, skip, grad, up):
    tokens, width = skip.shape
    low = up.shape[0]
    return pl.pallas_call(
        norm_kernel,
        out_shape=(
            pltpu.VMEM((tokens, 128), F32),
            pltpu.VMEM((tokens, low), BF16),
            pltpu.VMEM((low, tokens), BF16),
        ),
        in_specs=[SMEM, VMEM, VMEM, VMEM],
        out_specs=[VMEM] * 3,
        compiler_params=params(),
        cost_estimate=cost(2.5),
        name="norm",
    )(slots_local, skip, grad, up)


def terms_kernel(fsdp, slot_ref, place_ref, skip_ref, grad_ref, inv_ref, scale_ref, turned_ref, own_ref, *rest):
    far_refs, rest = rest[: 2 * (fsdp - 1)], rest[2 * (fsdp - 1) :]
    keep_out, send_out, hidden_ref, down_ref, up_ref = rest
    outs = (keep_out, send_out)
    core = place_ref[0]
    tokens, width = skip_ref.shape
    n = width // fsdp
    half = n // 2
    low = turned_ref.shape[0]
    first = core == 0
    inverse = inv_ref[...]
    projected = jnp.zeros((tokens, low), F32)
    for r in range(fsdp):
        start = lax.rem(place_ref[1] + r, fsdp) * n
        if r == 0:
            down = own_ref[...]
        else:
            mine, theirs = far_refs[r - 1][...], far_refs[fsdp - 1 + r - 1][...]
            down_ref[:half, :] = jnp.where(first, mine, theirs)
            down_ref[half:, :] = jnp.where(first, theirs, mine)
            down = down_ref[...]
        for j in range(n // 128):
            cols = pl.ds(pl.multiple_of(start + j * 128, 128), 128)
            hidden_ref[r, :, j * 128 : (j + 1) * 128] = (skip_ref[:, cols].astype(F32) * inverse * scale_ref[:, cols]).astype(BF16)
        term = jnp.dot(turned_ref[...], hidden_ref[r], preferred_element_type=F32)
        low_half, high_half = term[:, :half], term[:, half:]
        keep_out[r, :, :half] = jnp.where(first, low_half, high_half)
        send_out[r, :, :half] = jnp.where(first, high_half, low_half)
        projected += jnp.dot(hidden_ref[r], down, preferred_element_type=F32)
    count = slot_ref.shape[0]
    mask = member_mask([slot_ref[s] for s in range(count)], tokens // count, (tokens, low), 0)
    projected = jnp.where(mask, projected, 0.0).astype(BF16)
    up_ref[...] = tn_dot(projected, grad_ref[...])
    for r in range(fsdp):
        shard = lax.rem(place_ref[1] + r, fsdp)
        for h in range(2):
            at = pl.multiple_of((shard * 2 + (core ^ h)) * 128, 128)
            outs[h][r, :, half:] = up_ref[:, pl.ds(at, 128)]


def terms_call(slots_local, place, skip, inv, scales, turned, down, keep, other, grad):
    tokens, width = skip.shape
    low = turned.shape[0]
    n = down.shape[0]
    fsdp = width // n
    both = n // 2 + 128
    out = jax.ShapeDtypeStruct((fsdp, low, both), F32)
    return pl.pallas_call(
        functools.partial(terms_kernel, fsdp),
        out_shape=(out, out),
        in_specs=[SMEM, SMEM] + [VMEM] * (6 + 2 * (fsdp - 1)),
        out_specs=[VMEM] * 2,
        scratch_shapes=[
            pltpu.VMEM((fsdp, tokens, n), BF16),
            pltpu.VMEM((n, low), BF16),
            pltpu.VMEM((low, grad.shape[1]), F32),
        ],
        compiler_params=params(),
        cost_estimate=cost(7.5),
        name="terms",
    )(slots_local, place, skip, grad, inv, scales, turned, down, *keep, *other)


def base_kernel(r, fsdp, spans, place_ref, grad_ref, mid_ref, skip_ref, scale_ref, *rest):
    *ins, out_ref, sum_ref, both_ref, down_ref = rest
    tokens, n = out_ref.shape
    kdim = grad_ref.shape[1]
    core = place_ref[0]
    start = lax.rem(place_ref[1] + r, fsdp) * n
    half = n // 2
    if r:
        for j in range(kdim // 128):
            at = pl.multiple_of((place_ref[2] ^ j) * 128, 128)
            both_ref[:, j * 128 : (j + 1) * 128] = grad_ref[:, pl.ds(at, 128)]
        mine, theirs = ins[-2][...], ins[-1][...]
        down_ref[:half, :] = jnp.where(core == 0, mine, theirs)
        down_ref[half:, :] = jnp.where(core == 0, theirs, mine)
    else:
        both_ref[:, :kdim] = grad_ref[...]
        down_ref[...] = ins[1][...]
    both_ref[:, kdim:] = mid_ref[...]
    total = jnp.zeros(sum_ref.shape, F32)
    for i in range(n // COLUMNS):
        rows = slice(i * COLUMNS, (i + 1) * COLUMNS)
        parts = [ref[first + rows.start : first + rows.stop, :] for ref, first in zip(ins, spans)]
        weight = jnp.concatenate(parts + [down_ref[rows, :]], axis=-1)
        scale = scale_ref[:, pl.ds(pl.multiple_of(start + i * COLUMNS, 128), COLUMNS)]
        scaled = nt_dot(both_ref[...], weight) * scale
        out_ref[:, rows] = scaled.astype(BF16)
        for j in range(COLUMNS // 128):
            cols = pl.ds(pl.multiple_of(start + i * COLUMNS + j * 128, 128), 128)
            total += scaled[:, j * 128 : (j + 1) * 128] * skip_ref[:, cols].astype(F32)
    sum_ref[...] = total


def base_call(r, fsdp, place, grad, mid, skip, scales, spans, ins):
    tokens, kdim = grad.shape
    low = mid.shape[1]
    n = skip.shape[1] // fsdp
    return pl.pallas_call(
        functools.partial(base_kernel, r, fsdp, spans),
        out_shape=(pltpu.VMEM((tokens, n), BF16), pltpu.VMEM((tokens, 128), F32)),
        in_specs=[SMEM] + [VMEM] * (4 + len(ins)),
        out_specs=[VMEM] * 2,
        scratch_shapes=[
            pltpu.VMEM((tokens, kdim + low), BF16),
            pltpu.VMEM((n, low), BF16),
        ],
        compiler_params=params(),
        cost_estimate=cost(3.4),
        name="base",
    )(place, grad, mid, skip, scales, *ins)


def residual_kernel(fsdp, slot_ref, place_ref, skip_ref, inv_ref, *rest):
    base_refs, sum_refs, rest = rest[:fsdp], rest[fsdp : 2 * fsdp], rest[2 * fsdp :]
    out_hbm, done_ref, out_ref, keep_ref, pull_ref, sems = rest
    tokens, width = skip_ref.shape
    n = width // fsdp
    rows = tokens // slot_ref.shape[0]
    copies = Copies(sems)
    inverse = inv_ref[...]
    total = sum_refs[0][...]
    for ref in sum_refs[1:]:
        total = total + ref[...]
    mean = jnp.sum(total, axis=-1, keepdims=True) * inverse / width
    pull_ref[...] = mean * inverse
    for s in range(slot_ref.shape[0]):
        local = slot_ref[s]
        alive = jnp.logical_and(local >= 0, local < place_ref[3])
        at = slice(s * rows, (s + 1) * rows)
        keep_ref[at, :] = inverse[at, :] * jnp.where(alive, 1.0, 0.0)
    done_ref[...] = jnp.zeros_like(done_ref)
    stores = []
    for first in range(0, tokens, ROWS):

        def some_rows(k, carry):
            at = pl.ds(pl.multiple_of(first + k * 32, 32), 32)
            for r in range(fsdp):
                start = lax.rem(place_ref[1] + r, fsdp) * n
                for j in range(n // 128):
                    cols = pl.ds(pl.multiple_of(start + j * 128, 128), 128)
                    wide = skip_ref[at, cols].astype(F32)
                    scaled = base_refs[r][at, j * 128 : (j + 1) * 128].astype(F32)
                    out_ref[at, cols] = ((scaled - wide * pull_ref[at, :]) * keep_ref[at, :]).astype(BF16)
            return carry

        lax.fori_loop(0, ROWS // 32, some_rows, 0)
        at = pl.ds(first, ROWS)
        stores += copies.start([(out_ref.at[at, q], out_hbm.at[at, q]) for q in quarters(width)])
    wait(stores)


def residual_call(slots_local, place, skip, inv, bases, sums):
    tokens, width = skip.shape
    fsdp = len(bases)
    small = pltpu.VMEM((tokens, 128), F32)
    return pl.pallas_call(
        functools.partial(residual_kernel, fsdp),
        out_shape=(jax.ShapeDtypeStruct(skip.shape, BF16), jax.ShapeDtypeStruct((8, 128), F32)),
        in_specs=[SMEM, SMEM] + [VMEM] * (2 + 2 * fsdp),
        out_specs=(HBM, VMEM),
        scratch_shapes=[
            pltpu.VMEM((tokens, width), BF16),
            small,
            small,
            pltpu.SemaphoreType.DMA((4 * (tokens // ROWS),)),
        ],
        compiler_params=params(),
        cost_estimate=cost(4.7),
        name="residual",
    )(slots_local, place, skip, inv, *bases, *sums)


def both_kernel(keep_ref, got_ref, *out_refs):
    for r, ref in enumerate(out_refs):
        ref[...] = (keep_ref[r] + got_ref[r]).astype(ref.dtype)


def both_call(keep, got):
    fsdp, low, both = keep.shape
    held = jax.ShapeDtypeStruct((low, both), F32)
    return pl.pallas_call(
        both_kernel,
        out_shape=(held,) * (fsdp - 1) + (jax.ShapeDtypeStruct((low, both), BF16),),
        in_specs=[VMEM] * 2,
        out_specs=[VMEM] * fsdp,
        compiler_params=params(),
        cost_estimate=cost(0.4),
        name="both",
    )(keep, got)


def add_kernel(held_ref, got_ref, out_ref):
    out_ref[...] = (held_ref[...] + got_ref[...].astype(F32)).astype(BF16)


def add_call(held, got):
    return pl.pallas_call(
        add_kernel,
        out_shape=jax.ShapeDtypeStruct(held.shape, BF16),
        in_specs=[VMEM] * 2,
        out_specs=VMEM,
        compiler_params=params(),
        cost_estimate=cost(0.4),
        name="add",
    )(held, got)


def finish_kernel(slot_ref, held_ref, got_ref, done_ref, down_ref, up_ref):
    del done_ref
    total = held_ref[...] + got_ref[...].astype(F32)
    low = total.shape[0]
    member = lax.broadcasted_iota(jnp.int32, (low, 128), 0) // LOW_DIM
    counts = jnp.zeros((low, 128), F32)
    for s in range(slot_ref.shape[0]):
        counts += jnp.where(member == slot_ref[s], 1.0, 0.0)
    inverse = 1.0 / (BLOCK * counts)
    half = down_ref.shape[0]
    for j in range(half // 128):
        cols = slice(j * 128, (j + 1) * 128)
        down_ref[cols, :] = (total[:, cols] * inverse).T
    up_ref[...] = total[:, half:] * inverse


def finish_call(slots_local, held, got, done):
    low, both = held.shape
    half = both - 128
    return pl.pallas_call(
        finish_kernel,
        out_shape=(jax.ShapeDtypeStruct((half, low), F32), jax.ShapeDtypeStruct((low, 128), F32)),
        in_specs=[SMEM] + [VMEM] * 3,
        out_specs=[VMEM] * 2,
        compiler_params=params(),
        cost_estimate=cost(1.5),
        name="finish",
    )(slots_local, held, got, done)


SWAP = [(0, 1), (1, 0)]


def after(value, *deps):
    return lax.optimization_barrier((value, *deps))[0]


def per_device_square(
    fsdp,
    skip_stream,
    grad_stream,
    weight,
    down,
    up,
    scales,
    assignee,
):
    z = lax.axis_index("fsdp")
    c = lax.axis_index("dp")
    m = lax.axis_index("member")
    piece = c * 4 + lax.axis_index("parts") * 2 + m
    half = down.shape[0] // 2
    low = up.shape[0]
    members = low // LOW_DIM
    skip = skip_stream.reshape(-1, skip_stream.shape[2])
    grad = grad_stream.reshape(-1, grad_stream.shape[2])
    scale_row = scales[None, :]
    local = assignee - m * members
    place = jnp.stack([c, z, piece, jnp.int32(members)])

    shift = lambda v, r: lax.ppermute(v, "fsdp", [(i, (i + r) % fsdp) for i in range(fsdp)])
    over = lambda v, axis: lax.ppermute(v, axis, SWAP)
    gate = lax.optimization_barrier
    n = down.shape[0]

    def base(r, spans, ins):
        return base_call(r, fsdp, place, grad, mid, skip, scale_row, spans, ins)

    def core(value):
        return over(value, "dp")

    unit = lax.dynamic_slice_in_dim(weight, piece * 128, 128, 1)
    down_half = lax.dynamic_slice_in_dim(down, c * half, half, 0)
    u1, u3 = shift(unit, -1), shift(unit, 1)
    inv, mid, turned = norm_call(local, skip, grad, up)
    u1, u3, down_half, inv, mid, turned = gate((u1, u3, down_half, inv, mid, turned))

    u = jnp.concatenate([u1, u3], axis=0)
    x, y = over(u, "member"), over(u, "parts")
    keep = [shift(down_half, -r) for r in range(1, fsdp)]
    base0, sum0 = base(0, (0,), (weight, down))
    u, x, y, keep, u3, sum0 = gate((u, x, y, keep, u3, sum0))

    u2 = shift(u3, 1)
    d1, d3 = over(x[:n], "parts"), over(y[n:], "member")
    other = [core(v) for v in keep]
    far_u, far_x, far_y = core(u), core(x), core(y)
    turned, far_u, far_x, far_y = gate((turned, far_u, far_x, far_y))
    terms = terms_call(local, place, skip, inv, scale_row, turned, down, keep, other, grad)
    d1, d3, far_u, far_x, far_y, terms, u2 = gate((d1, d3, far_u, far_x, far_y, terms, u2))

    *held, sent = both_call(terms[0], core(terms[1]))
    x2, y2 = over(u2, "member"), over(u2, "parts")
    got = shift(sent, 1)
    base1, sum1 = base(1, (0, 0, 0, 0) * 2, (u, x, y, d1, far_u, far_x, far_y, core(d1), keep[0], other[0]))
    u2, x2, y2, d3, got, sum1 = gate((u2, x2, y2, d3, got, sum1))

    d2 = over(x2, "parts")
    got = shift(add_call(held[2], got), 1)
    far2 = [core(v) for v in (u2, x2, y2)]
    base3, sum3 = base(3, (n, n, n, 0) * 2, (u, x, y, d3, far_u, far_x, far_y, core(d3), keep[2], other[2]))
    d2, far2, sum3 = gate((d2, far2, sum3))

    got = shift(add_call(held[1], got), 1)
    base2, sum2 = base(2, (0,) * 8, (u2, x2, y2, d2, *far2, core(d2), keep[1], other[1]))
    residual, done = residual_call(local, place, skip, inv, (base0, base1, base2, base3), (sum0, sum1, sum2, sum3))
    grad_down, grad_up = finish_call(local, held[0], got, done)
    return residual.reshape(skip_stream.shape), grad_down, grad_up


def solution(mesh):
    placed = (
        P(("parts", "member"), ("fsdp", "dp"), None),
        P(("parts", "member"), ("fsdp", "dp"), None),
        P("fsdp", None),
        P("fsdp", ("parts", "member")),
        P(("parts", "member"), None),
        P(),
        P(("parts", "member")),
    )
    sizes = dict(mesh.shape)
    square = sizes["parts"] == 2 and sizes["member"] == 2 and sizes["dp"] == 2 and sizes["fsdp"] == 4
    return jax.shard_map(
        functools.partial(per_device_square, sizes["fsdp"]) if square else per_device_any,
        mesh=mesh,
        in_specs=placed,
        out_specs=(
            P(("parts", "member"), ("fsdp", "dp"), None),
            P(("fsdp", "dp"), ("parts", "member")),
            P(("parts", "member"), ("fsdp", "dp")),
        ),
        check_vma=False,
    )
```
